256 devices in a mesh: scan: 64 (over x, z, core), tile: 4 (over y).
Axes of the slice: x: 4, y: 4, z: 8, core: 2. Of those that a mesh axis runs over, the one named last changes fastest.
Arguments:
- object_field: float32 [2, 2048, 1024], P(None, 'scan', 'tile'), may hold values from -4.2 to 4.2
- probe: float32 [2, 3, 256, 256], replicated, may hold values from -1.8 to 1.8
- amplitude: float32 [512, 256, 256], P(('scan', 'tile')), may hold values from 0.3 to 3
- positions: int32 [512, 2], replicated, may hold values from -128 to 1919, as said below
- scan_list: int32 [512], P(('scan', 'tile')), may hold values from 0 to 511, as said below
Outputs:
- updated_object: float32 [2, 2048, 1024], P(None, 'scan', 'tile')
- updated_probe: float32 [2, 3, 256, 256], replicated
The draws below stay inside these ranges and needn't reach their ends.
Inputs may be any that keep to these rules, and one draw needn't show every extreme that they name: positions[k, 0] is a row offset and positions[k, 1] a column offset; column offsets lie in 0 to 768. The position in a slot held by the device with scan index s has a row offset r with s * 32 - 256/2 <= r < (s + 1) * 32 - 256/2. `scan_list`: each position appears in exactly one slot.
All inputs are finite; a program needn't handle non-finite values.
Results may differ from the reference program's by a relative error of at most 0.0001.
Values sent between devices are 32-bit elements; how exact they have to be, the bound alone decides.
A program may use at most 64 MiB of HBM per device.

```python
import math
import jax
import jax.numpy as jnp
from jax import lax

PATCH = 256
MODES = 3
TILE_ROWS = 32
POSITIONS_DEV = 2
ITERATIONS = 2
OBJECT_ROWS = 2048
OBJECT_COLS = 1024
POSITIONS = 512
N_TILE = 4


def slot_plan(key):
    slots = jnp.arange(POSITIONS, dtype=jnp.int32)
    strips = slots // (POSITIONS_DEV * N_TILE)
    key_rows, key_columns, key_order = jax.random.split(key, 3)
    within = jax.random.randint(key_rows, (POSITIONS,), 0, TILE_ROWS, dtype=jnp.int32)
    columns = jax.random.randint(key_columns, (POSITIONS,), 0, OBJECT_COLS - PATCH + 1, dtype=jnp.int32)
    within = within.at[0].set(0).at[POSITIONS - 1].set(TILE_ROWS - 1)
    columns = columns.at[0].set(0).at[POSITIONS - 1].set(OBJECT_COLS - PATCH)
    rows = strips * TILE_ROWS + within - PATCH // 2
    order = jax.random.permutation(key_order, POSITIONS).astype(jnp.int32)
    table = jnp.zeros((POSITIONS, 2), jnp.int32).at[order].set(jnp.stack([rows, columns], axis=1))
    return (table, order)


def draw_positions(key, part):
    table, order = slot_plan(key)
    return table


def draw_scan_list(key, part):
    table, order = slot_plan(key)
    return order


def block_levels(rng, dims, shards, low, high):
    gain = 1.0
    for axis_at, parts in shards:
        draws = jax.random.uniform(jax.random.fold_in(jax.random.fold_in(rng, 6), axis_at), (parts,), jnp.float32, low / len(shards), high / len(shards))
        gain = gain * jnp.repeat(jnp.exp(draws), dims[axis_at] // parts).reshape((-1,) + (1,) * (len(dims) - 1 - axis_at))
    return gain


def gaussian(rng, extent, scale, bound, cuts=(), held_as=jnp.bfloat16):
    gain = block_levels(rng, extent, cuts, -0.22, 0.18) if cuts else 1.0
    result = jax.random.normal(rng, extent, jnp.float32) * scale * gain
    return jnp.minimum(jnp.maximum(result, -bound), bound).astype(held_as)


def setup_inputs(seed: int = 0) -> dict:
    keys = jax.random.split(jax.random.key(seed), 6)
    return {
        "object_field": gaussian(keys[0], (2, OBJECT_ROWS, OBJECT_COLS), 0.7, 4.2, ((1, 64), (2, 4)), jnp.float32),
        "probe": gaussian(keys[1], (2, MODES, PATCH, PATCH), 0.3, 1.8, (), jnp.float32),
        "amplitude": jnp.clip(jnp.exp(math.log(3.0) - 2.3025851 * jax.random.uniform(keys[2], (POSITIONS, PATCH, PATCH), jnp.float32) ** block_levels(keys[2], (POSITIONS, PATCH, PATCH), ((0, 256),), -0.2, 0.2)), 0.3, 3.0),
        "positions": draw_positions(jax.random.fold_in(keys[5], 71), 0),
        "scan_list": draw_scan_list(jax.random.fold_in(keys[5], 71), 0),
    }


INTENSITY_FLOOR = 0.1
OBJECT_RATE = 0.05
PROBE_RATE = 0.5

def reference(object_field, probe, amplitude, positions, scan_list):
    margin = PATCH // 2
    field = lax.complex(object_field[0], object_field[1])
    modes = lax.complex(probe[0], probe[1])
    row_start = (positions[scan_list, 0] + margin).astype(jnp.int32)
    column_start = positions[scan_list, 1].astype(jnp.int32)
    for rounds in range(ITERATIONS):
        padded = jnp.pad(field, ((margin, margin), (0, 0)))

        def visit(carry, item):
            grad_field, grad_modes = carry
            pattern, row_at, column_at = item
            patch = lax.dynamic_slice(padded, (row_at, column_at), (PATCH, PATCH))
            far = jnp.fft.fft2(modes * patch[None], norm='ortho')
            power = lax.optimization_barrier(jnp.sum(far.real * far.real + far.imag * far.imag, axis=0))
            factor = 1.0 - pattern / jnp.sqrt(jnp.maximum(power, INTENSITY_FLOOR))
            back = jnp.fft.ifft2(far * factor[None], norm='ortho')
            term = lax.optimization_barrier(jnp.sum(jnp.conj(modes) * back, axis=0))
            previous = lax.dynamic_slice(grad_field, (row_at, column_at), (PATCH, PATCH))
            grad_field = lax.dynamic_update_slice(grad_field, previous + term, (row_at, column_at))
            grad_modes = grad_modes + jnp.conj(patch)[None] * back
            return ((grad_field, grad_modes), None)
        start = (jnp.zeros_like(padded), jnp.zeros_like(modes))
        (grad_field, grad_modes), unused = lax.scan(visit, start, (amplitude, row_start, column_start))
        field = field - OBJECT_RATE * grad_field[margin:margin + OBJECT_ROWS]
        modes = modes - PROBE_RATE / POSITIONS * grad_modes
    return (jnp.stack([field.real, field.imag]), jnp.stack([modes.real, modes.imag]))
```

```python
import functools
import math

import jax
import jax.numpy as jnp
import ml_dtypes
import numpy as np
from jax import lax
from jax.experimental import pallas as pl
from jax.experimental.pallas import tpu as pltpu
from jax.sharding import PartitionSpec as P

ITERATIONS = 2
INTENSITY_FLOOR = 0.1
OBJECT_RATE = 0.05
PROBE_RATE = 0.5

CORES = 2
CHIPS_Z = 8
LANES = 128
MESH = pl.DeviceIdType.MESH
VMEM_LIMIT = 48 * 1024 * 1024


def dft_tables(length):
    index = np.arange(length)
    angle = (np.outer(index, index) % length) * (-2.0 * math.pi / length)
    scale = 1.0 / math.sqrt(length)
    cosine, sine = np.cos(angle) * scale, np.sin(angle) * scale
    forward = np.block([[cosine, sine], [-sine, cosine]])
    tables = []
    for table in (forward, forward.T):
        high = table.astype(ml_dtypes.bfloat16)
        low = (table - high.astype(np.float64)).astype(ml_dtypes.bfloat16)
        tables += [high, low]
    return np.stack(tables)


def halves(values):
    high = values.astype(jnp.bfloat16)
    low = (values - high.astype(jnp.float32)).astype(jnp.bfloat16)
    return high, low


def product(left, right):
    dot = functools.partial(jnp.dot, preferred_element_type=jnp.float32)
    return dot(left[0], right[0]) + (dot(left[0], right[1]) + dot(left[1], right[0]))


def sublane(shape):
    return lax.broadcasted_iota(jnp.int32, shape, 1)


def read_rows(values, inside):
    turned = pltpu.roll(values, lax.rem(8 - inside, 8), 1)
    return jnp.where(sublane(turned[1:].shape) < 8 - inside, turned[:-1], turned[1:])


def place_rows(values, inside):
    turned = pltpu.roll(values, inside, 1)
    edge = jnp.zeros((1,) + values.shape[1:], values.dtype)
    before = jnp.concatenate([edge, turned], axis=0)
    after = jnp.concatenate([turned, edge], axis=0)
    return jnp.where(sublane(before.shape) < inside, before, after)


def slots_kernel(
    rows_ref, window_ref, modes_ref, amplitude_ref, table_ref, grad_ref, grad_modes_ref, patch_ref
):
    slots, _, band, patch = window_ref.shape
    count = modes_ref.shape[1]
    forward = (table_ref[0], table_ref[1])
    inverse = (table_ref[2], table_ref[3])
    margin = band - patch
    for slot in range(slots):
        row = rows_ref[slot]
        first = pl.multiple_of((row // 8) * 8, 8)
        inside = row - first
        for part in range(2):
            rows = window_ref[slot, part, pl.ds(first, patch + 8), :].reshape(patch // 8 + 1, 8, patch)
            patch_ref[part] = read_rows(rows, inside).reshape(patch, patch)
            grad_ref[slot, part, :margin, :] = jnp.zeros((margin, patch), jnp.float32)
            grad_ref[slot, part, patch:, :] = jnp.zeros((margin, patch), jnp.float32)
        power = None
        far = []
        for m in range(count):
            patch_real, patch_imag = patch_ref[0], patch_ref[1]
            mode_real, mode_imag = modes_ref[0, m], modes_ref[1, m]
            wave = jnp.concatenate(
                [
                    mode_real * patch_real - mode_imag * patch_imag,
                    mode_real * patch_imag + mode_imag * patch_real,
                ],
                axis=1,
            )
            right = product(halves(wave), forward)
            right = jnp.concatenate([right[:, :patch], right[:, patch:]], axis=0)
            left = product(inverse, halves(right))
            far.append(left)
            square = left * left
            square = square[:patch] + square[patch:]
            power = square if power is None else power + square
        factor = 1.0 - amplitude_ref[slot] * lax.rsqrt(jnp.maximum(power, INTENSITY_FLOOR))
        factor = jnp.concatenate([factor, factor], axis=0)
        term_real = term_imag = None
        for m in range(count):
            left = product(forward, halves(far[m] * factor))
            left = jnp.concatenate([left[:patch], left[patch:]], axis=1)
            back = product(halves(left), inverse)
            back_real, back_imag = back[:, :patch], back[:, patch:]
            patch_real, patch_imag = patch_ref[0], patch_ref[1]
            mode_real, mode_imag = modes_ref[0, m], modes_ref[1, m]
            real = mode_real * back_real + mode_imag * back_imag
            imag = mode_real * back_imag - mode_imag * back_real
            term_real = real if term_real is None else term_real + real
            term_imag = imag if term_imag is None else term_imag + imag
            probe_real = patch_real * back_real + patch_imag * back_imag
            probe_imag = patch_real * back_imag - patch_imag * back_real
            if slot == 0:
                grad_modes_ref[0, m] = probe_real
                grad_modes_ref[1, m] = probe_imag
            else:
                grad_modes_ref[0, m] += probe_real
                grad_modes_ref[1, m] += probe_imag
        for part, term in enumerate((term_real, term_imag)):
            term = place_rows(term.reshape(patch // 8, 8, patch), inside)
            grad_ref[slot, part, pl.ds(first, patch + 8), :] = term.reshape(patch + 8, patch)


def slot_gradients(rows, windows, modes, amplitude, tables):
    slots, _, band, patch = windows.shape
    count = modes.shape[1]
    vmem = pl.BlockSpec(memory_space=pltpu.VMEM)
    return pl.pallas_call(
        slots_kernel,
        out_shape=(
            jax.ShapeDtypeStruct(windows.shape, jnp.float32),
            jax.ShapeDtypeStruct(modes.shape, jnp.float32),
        ),
        in_specs=[pl.BlockSpec(memory_space=pltpu.SMEM), vmem, vmem, vmem, vmem],
        out_specs=(vmem, vmem),
        scratch_shapes=[pltpu.VMEM((2, patch, patch), jnp.float32)],
        compiler_params=pltpu.CompilerParams(vmem_limit_bytes=VMEM_LIMIT),
        cost_estimate=pl.CostEstimate(
            flops=slots * count * 48 * 2 * patch**3,
            bytes_accessed=4 * (2 * windows.size + 2 * modes.size + amplitude.size),
            transcendentals=slots * patch * patch,
        ),
    )(rows, windows, modes, amplitude, tables)


class Place:
    def __init__(self, chips_z):
        self.scan = lax.axis_index("scan")
        self.tile = lax.axis_index("tile")
        self.scans = lax.axis_size("scan")
        self.tiles = lax.axis_size("tile")
        self.chips_z = chips_z
        self.chips_x = self.scans // (chips_z * CORES)
        self.core = lax.rem(self.scan, CORES)
        self.z = lax.rem(self.scan // CORES, chips_z)
        self.x = self.scan // (CORES * chips_z)

    def at_core(self):
        return (self.scan + 1 - 2 * self.core, self.tile)

    def ring_x(self, k):
        x = lax.rem(self.x + k, self.chips_x)
        return x, ((x * self.chips_z + self.z) * CORES + self.core, self.tile)

    def ring_z(self, k):
        z = lax.rem(self.z + k, self.chips_z)
        return z, ((self.x * self.chips_z + z) * CORES + self.core, self.tile)

    def ring_tile(self, k):
        tile = lax.rem(self.tile + k, self.tiles)
        return tile, (self.scan, tile)

    def near(self, d):
        other = self.scan + d
        return jnp.logical_and(other >= 0, other < self.scans), (other, self.tile)


def distances(reach):
    far_first = sorted(range(1, reach + 1), reverse=True)
    return [sign * d for d in far_first for sign in (1, -1)]


def greet(partners):
    barrier = pltpu.get_barrier_semaphore()
    total = 0
    for condition, device in partners:
        if condition is None:
            pl.semaphore_signal(barrier, inc=1, device_id=device, device_id_type=MESH)
            total = total + 1
        else:

            @pl.when(condition)
            def _(device=device):
                pl.semaphore_signal(barrier, inc=1, device_id=device, device_id_type=MESH)

            total = total + condition.astype(jnp.int32)
    pl.semaphore_wait(barrier, total)


def remote(src, dst, sems, at, device):
    return pltpu.make_async_remote_copy(
        src_ref=src,
        dst_ref=dst,
        send_sem=sems[0].at[at],
        recv_sem=sems[1].at[at],
        device_id=device,
        device_id_type=MESH,
    )


def gather_kernel(reach, chips_z, exchange, *refs):
    if exchange:
        (field_ref, columns_ref, window_ref, table_ref, strip, outgoing, columns, tile_send, tile_recv,
         scan_send, scan_recv, column_send, column_recv, local_sem) = refs
    else:
        (field_ref, columns, window_ref, strip, outgoing, tile_send, tile_recv, scan_send, scan_recv) = refs
    place = Place(chips_z)
    _, rows, width = field_ref.shape
    order = distances(reach)
    tile_sems, scan_sems = (tile_send, tile_recv), (scan_send, scan_recv)
    greet(
        [(None, place.ring_tile(k)[1]) for k in range(1, place.tiles)]
        + [place.near(d) for d in order]
    )
    own = pl.ds(pl.multiple_of(place.tile * width, LANES), width)
    gathers = [
        remote(field_ref, strip.at[:, :, own], tile_sems, k - 1, place.ring_tile(k)[1])
        for k in range(1, place.tiles)
    ]
    for copy in gathers:
        copy.start()
    notes = []
    if exchange:
        table_ref[reach] = columns_ref[...]
        for at, d in enumerate(order):
            exists, device = place.near(d)
            note = remote(columns_ref, table_ref.at[reach - d], (column_send, column_recv), at, device)
            pl.when(exists)(note.start)
            notes.append((exists, place.near(-d)[0], note))
    strip[:, :, own] = field_ref[...]
    pad = strip.shape[2] - width * place.tiles
    strip[:, :, width * place.tiles :] = jnp.zeros((2, rows, pad), jnp.float32)
    for at, d in enumerate(order):
        exists, _ = place.near(-d)

        @pl.when(jnp.logical_not(exists))
        def _(d=d):
            window_ref[:, :, (reach - d) * rows : (reach - d + 1) * rows, :] = jnp.zeros(
                (window_ref.shape[0], 2, rows, window_ref.shape[3]), jnp.float32
            )
            if exchange:
                table_ref[reach - d] = jnp.zeros(columns_ref.shape, jnp.int32)

    for exists, from_exists, note in notes:
        pl.when(exists)(note.wait_send)
        pl.when(from_exists)(note.wait_recv)
    if exchange:
        local = pltpu.make_async_copy(table_ref, columns, local_sem)
        local.start()
        local.wait()
    for copy in gathers:
        copy.wait()

    lane = lax.broadcasted_iota(jnp.int32, (rows, LANES), 1)

    def cut(at, target):
        for slot in range(window_ref.shape[0]):
            column = columns[at, 0, slot] if exchange else columns[at, slot]
            first = column // LANES
            inside = column - first * LANES
            for part in range(2):
                pieces = []
                for i in range(width // LANES + 1):
                    piece = strip[part, :, LANES * i : LANES * (i + 1)]
                    for block in range(1, (place.tiles - 1) * width // LANES + 1):
                        at_block = strip[part, :, LANES * (block + i) : LANES * (block + i + 1)]
                        piece = jnp.where(first == block, at_block, piece)
                    pieces.append(pltpu.roll(piece, lax.rem(LANES - inside, LANES), 1))
                for i in range(width // LANES):
                    target[slot, part, :, LANES * i : LANES * (i + 1)] = jnp.where(
                        lane < LANES - inside, pieces[i], pieces[i + 1]
                    )

    sends = []
    for at, d in enumerate(order):
        exists, device = place.near(d)
        copy = remote(
            outgoing.at[at],
            window_ref.at[:, :, (reach - d) * rows : (reach - d + 1) * rows, :],
            scan_sems,
            at,
            device,
        )

        @pl.when(exists)
        def _(at=at, d=d, copy=copy):
            cut(reach + d, outgoing.at[at])
            copy.start()

        sends.append((exists, place.near(-d)[0], copy))
    cut(reach, window_ref.at[:, :, reach * rows : (reach + 1) * rows, :])
    for exists, from_exists, copy in sends:
        pl.when(exists)(copy.wait_send)
        pl.when(from_exists)(copy.wait_recv)


def gather_windows(field, columns, reach, slots, patch, chips_z, exchange, collective_id):
    _, rows, width = field.shape
    tiles = lax.axis_size("tile")
    vmem = pl.BlockSpec(memory_space=pltpu.VMEM)
    smem = pl.BlockSpec(memory_space=pltpu.SMEM)
    near = 2 * reach
    dma = pltpu.SemaphoreType.DMA
    window = jax.ShapeDtypeStruct((slots, 2, (near + 1) * rows, patch), jnp.float32)
    scratch = [
        pltpu.VMEM((2, rows, width * tiles + LANES), jnp.float32),
        pltpu.VMEM((near, slots, 2, rows, patch), jnp.float32),
    ]
    sems = [dma((tiles - 1,)), dma((tiles - 1,)), dma((near,)), dma((near,))]
    if exchange:
        table = (near + 1,) + columns.shape
        out_shape = (window, jax.ShapeDtypeStruct(table, jnp.int32))
        out_specs = (vmem, vmem)
        scratch += [pltpu.SMEM(table, jnp.int32)] + sems + [dma((near,)), dma((near,)), dma(())]
    else:
        out_shape, out_specs = window, vmem
        scratch += sems
    return pl.pallas_call(
        functools.partial(gather_kernel, reach, chips_z, exchange),
        out_shape=out_shape,
        in_specs=[vmem, vmem if exchange else smem],
        out_specs=out_specs,
        scratch_shapes=scratch,
        compiler_params=pltpu.CompilerParams(
            collective_id=collective_id, has_side_effects=True, vmem_limit_bytes=VMEM_LIMIT
        ),
    )(field, columns)


def reduce_kernel(
    reach, chips_z, owners, rate, columns, grad_ref, grad_modes_ref, field_ref, modes_ref,
    new_field_ref, new_modes_ref, arrived, strip, tile_parts, core_part, core_sum, x_parts, x_sum,
    y_parts, y_sum, z_parts, scan_send, scan_recv, tile_send, tile_recv, core_send, core_recv,
    x_send, x_recv, y_send, y_recv, z_send, z_recv, zg_send, zg_recv, yg_send, yg_recv,
    xg_send, xg_recv, cg_send, cg_recv,
):
    place = Place(chips_z)
    _, rows, width = field_ref.shape
    slots = grad_ref.shape[0]
    order = distances(reach)
    xs, ys, zs = place.chips_x, place.tiles, place.chips_z
    half = grad_modes_ref.shape[0] // CORES
    quarter = half // xs
    part = quarter // ys
    piece = part // owners
    owner = place.z < owners

    partners = [(None, place.at_core())]
    partners += [(None, place.ring_x(k)[1]) for k in range(1, xs)]
    partners += [(None, place.ring_tile(k)[1]) for k in range(1, ys)]
    for k in range(1, zs):
        z, device = place.ring_z(k)
        partners.append((jnp.logical_or(owner, z < owners), device))
    partners += [place.near(d) for d in order]
    greet(partners)

    def rows_at(start, size):
        return pl.ds(pl.multiple_of(start, 8), size)

    mine, other = place.core * half, (1 - place.core) * half
    core_copies = []
    for k in list(range(1, xs)) + [0]:
        x = lax.rem(place.x + k, xs)
        copy = remote(
            grad_modes_ref.at[rows_at(other + x * quarter, quarter)],
            core_part.at[rows_at(x * quarter, quarter)],
            (core_send, core_recv), k, place.at_core(),
        )
        copy.start()
        core_copies.append(copy)

    sends = []
    for at, d in enumerate(order):
        exists, device = place.near(d)
        copy = remote(
            grad_ref.at[:, :, (reach + d) * rows : (reach + d + 1) * rows, :],
            arrived.at[reach - d], (scan_send, scan_recv), at, device,
        )
        pl.when(exists)(copy.start)
        from_exists = place.near(-d)[0]

        @pl.when(jnp.logical_not(from_exists))
        def _(d=d):
            arrived[reach - d] = jnp.zeros(arrived.shape[1:], jnp.float32)

        sends.append((exists, from_exists, copy))

    x_copies = []
    for k, copy in zip(list(range(1, xs)) + [0], core_copies):
        copy.wait_recv()
        x, device = place.ring_x(k)
        at = rows_at(x * quarter, quarter)
        core_sum[at, :] = core_part[at, :] + grad_modes_ref[rows_at(mine + x * quarter, quarter), :]
        if k:
            copy = remote(core_sum.at[at], x_parts.at[k - 1], (x_send, x_recv), k - 1, device)
            copy.start()
            x_copies.append(copy)
    arrived[reach] = grad_ref[:, :, reach * rows : (reach + 1) * rows, :]
    for copy in x_copies:
        copy.wait_recv()
    total = core_sum[rows_at(place.x * quarter, quarter), :]
    for k in range(xs - 1):
        total = total + x_parts[k]
    x_sum[...] = total
    y_copies = []
    for k in range(1, ys):
        y, device = place.ring_tile(k)
        copy = remote(x_sum.at[rows_at(y * part, part)], y_parts.at[k - 1], (y_send, y_recv), k - 1, device)
        copy.start()
        y_copies.append(copy)
    for copy in y_copies:
        copy.wait_recv()
    total = x_sum[rows_at(place.tile * part, part), :]
    for k in range(ys - 1):
        total = total + y_parts[k]
    y_sum[...] = total
    z_copies = []
    for k in range(1, zs):
        z, device = place.ring_z(k)
        start = jnp.minimum(z, owners - 1) * piece
        copy = remote(y_sum.at[rows_at(start, piece)], z_parts.at[k - 1], (z_send, z_recv), k - 1, device)
        pl.when(z < owners)(copy.start)
        z_copies.append((z < owners, copy))

    for exists, from_exists, copy in sends:
        pl.when(from_exists)(copy.wait_recv)
    lane = lax.broadcasted_iota(jnp.int32, (rows, LANES), 1)
    blocks = width * ys // LANES
    strip[...] = jnp.zeros(strip.shape, jnp.float32)

    def place_window(index, carry):
        source, slot = index // slots, lax.rem(index, slots)
        column = columns[source, slot]
        first = column // LANES
        inside = column - first * LANES
        for p in range(2):
            values = [
                pltpu.roll(arrived[source, slot, p, :, LANES * i : LANES * (i + 1)], inside, 1)
                for i in range(width // LANES)
            ]
            values = [jnp.zeros_like(values[0])] + values + [jnp.zeros_like(values[0])]
            shifted = [
                jnp.where(lane < inside, values[i], values[i + 1]) for i in range(width // LANES + 1)
            ]
            for block in range(blocks):
                term = jnp.zeros_like(values[0])
                for i, value in enumerate(shifted):
                    term = jnp.where(first + i == block, value, term)
                strip[p, :, LANES * block : LANES * (block + 1)] += term
        return carry

    lax.fori_loop(0, arrived.shape[0] * slots, place_window, 0)
    tile_copies = []
    for k in range(1, ys):
        y, device = place.ring_tile(k)
        copy = remote(
            strip.at[:, :, pl.ds(pl.multiple_of(y * width, LANES), width)],
            tile_parts.at[k - 1], (tile_send, tile_recv), k - 1, device,
        )
        copy.start()
        tile_copies.append(copy)

    my_quarter = mine + place.x * quarter
    my_part = my_quarter + place.tile * part
    my_piece = jnp.minimum(place.z, owners - 1) * piece

    @pl.when(owner)
    def _():
        for _, copy in z_copies:
            copy.wait_recv()
        total = y_sum[rows_at(my_piece, piece), :]
        for k in range(zs - 1):
            total = total + z_parts[k]
        at = rows_at(my_part + my_piece, piece)
        new_modes_ref[at, :] = modes_ref[at, :] - rate * total

    gathers = []
    for k in range(1, zs):
        z, device = place.ring_z(k)
        ref = new_modes_ref.at[rows_at(my_part + my_piece, piece)]
        copy = remote(ref, ref, (zg_send, zg_recv), k - 1, device)
        pl.when(owner)(copy.start)
        gathers.append((owner, lax.rem(place.z + zs - k, zs) < owners, copy))
    for _, from_owner, copy in gathers:
        pl.when(from_owner)(copy.wait_recv)
    yg_copies = []
    for k in range(1, ys):
        ref = new_modes_ref.at[rows_at(my_part, part)]
        copy = remote(ref, ref, (yg_send, yg_recv), k - 1, place.ring_tile(k)[1])
        copy.start()
        yg_copies.append(copy)
    for copy in yg_copies:
        copy.wait_recv()
    xg_copies, cg_copies = [], []
    for k in range(1, xs):
        ref = new_modes_ref.at[rows_at(my_quarter, quarter)]
        copy = remote(ref, ref, (xg_send, xg_recv), k - 1, place.ring_x(k)[1])
        copy.start()
        xg_copies.append(copy)
    ref = new_modes_ref.at[rows_at(my_quarter, quarter)]
    copy = remote(ref, ref, (cg_send, cg_recv), 0, place.at_core())
    copy.start()
    cg_copies.append(copy)

    for copy in tile_copies:
        copy.wait_recv()
    total = strip[:, :, pl.ds(pl.multiple_of(place.tile * width, LANES), width)]
    for k in range(ys - 1):
        total = total + tile_parts[k]
    new_field_ref[...] = field_ref[...] - OBJECT_RATE * total

    for k, copy in zip(range(1, xs), xg_copies):
        copy.wait_recv()
        x = lax.rem(place.x + xs - k, xs)
        ref = new_modes_ref.at[rows_at(mine + x * quarter, quarter)]
        copy = remote(ref, ref, (cg_send, cg_recv), k, place.at_core())
        copy.start()
        cg_copies.append(copy)
    for copy in cg_copies:
        copy.wait()
    for copy in core_copies + x_copies + y_copies + tile_copies + yg_copies + xg_copies:
        copy.wait_send()
    for condition, copy in z_copies:
        pl.when(condition)(copy.wait_send)
    for condition, _, copy in gathers:
        pl.when(condition)(copy.wait_send)
    for exists, _, copy in sends:
        pl.when(exists)(copy.wait_send)


def reduce_gradients(columns, grad, grad_modes, field, modes, reach, chips_z, rate, collective_id):
    _, rows, width = field.shape
    slots, _, _, patch = grad.shape
    tiles, scans = lax.axis_size("tile"), lax.axis_size("scan")
    chips_x = scans // (CORES * chips_z)
    flat = (modes.size // patch, patch)
    half = flat[0] // CORES
    quarter = half // chips_x
    part = quarter // tiles
    owners = max(n for n in range(1, chips_z + 1) if part % (8 * n) == 0)
    piece = part // owners
    near = 2 * reach
    vmem = pl.BlockSpec(memory_space=pltpu.VMEM)
    f32 = functools.partial(pltpu.VMEM, dtype=jnp.float32)
    dma = pltpu.SemaphoreType.DMA
    counts = [near, tiles - 1, chips_x, chips_x - 1, tiles - 1, chips_z - 1, chips_z - 1, tiles - 1, chips_x - 1, chips_x]
    new_field, new_modes = pl.pallas_call(
        functools.partial(reduce_kernel, reach, chips_z, owners, rate),
        out_shape=(
            jax.ShapeDtypeStruct(field.shape, jnp.float32),
            jax.ShapeDtypeStruct(flat, jnp.float32),
        ),
        in_specs=[pl.BlockSpec(memory_space=pltpu.SMEM), vmem, vmem, vmem, vmem],
        out_specs=(vmem, vmem),
        scratch_shapes=[
            f32((near + 1, slots, 2, rows, patch)),
            f32((2, rows, width * tiles)),
            f32((tiles - 1, 2, rows, width)),
            f32((half, patch)),
            f32((half, patch)),
            f32((chips_x - 1, quarter, patch)),
            f32((quarter, patch)),
            f32((tiles - 1, part, patch)),
            f32((part, patch)),
            f32((chips_z - 1, piece, patch)),
        ]
        + [dma((n,)) for n in counts for _ in range(2)],
        compiler_params=pltpu.CompilerParams(
            collective_id=collective_id, has_side_effects=True, vmem_limit_bytes=VMEM_LIMIT
        ),
    )(columns, grad, grad_modes.reshape(flat), field, modes.reshape(flat))
    return new_field, new_modes.reshape(modes.shape)


def on_device(chips_z, object_field, probe, amplitude, positions, scan_list):
    tile_rows = object_field.shape[1]
    patch = probe.shape[2]
    reach = patch // (2 * tile_rows)
    total = positions.shape[0]
    slots = scan_list.shape[0]
    tables = jnp.asarray(dft_tables(patch))
    match = scan_list[:, None] == jnp.arange(total, dtype=jnp.int32)[None, :]
    found = jnp.sum(jnp.where(match[:, :, None], positions[None], 0), axis=1)
    row_start = found[:, 0] - lax.axis_index("scan") * tile_rows + patch // 2
    own_columns = jnp.zeros((8, LANES), jnp.int32).at[0, :slots].set(found[:, 1])
    field = object_field
    modes = probe
    columns = None
    for rounds in range(ITERATIONS):
        if rounds == 0:
            windows, table = gather_windows(field, own_columns, reach, slots, patch, chips_z, True, 1)
            columns = table[:, 0, :slots]
        else:
            windows = gather_windows(field, columns, reach, slots, patch, chips_z, False, 2)
        grad, grad_modes = slot_gradients(row_start, windows, modes, amplitude, tables)
        field, modes = reduce_gradients(
            columns, grad, grad_modes, field, modes, reach, chips_z, PROBE_RATE / total, 3
        )
    return (field, modes)


def solution(mesh, chips_z=CHIPS_Z):
    in_specs = (
        P(None, "scan", "tile"),
        P(),
        P(("scan", "tile"), None, None),
        P(),
        P(("scan", "tile")),
    )
    out_specs = (P(None, "scan", "tile"), P())
    return jax.shard_map(
        functools.partial(on_device, chips_z),
        mesh=mesh,
        in_specs=in_specs,
        out_specs=out_specs,
        check_vma=False,
    )
```

```python
import functools
import math

import jax
import jax.numpy as jnp
import ml_dtypes
import numpy as np
from jax import lax
from jax.experimental import pallas as pl
from jax.experimental.pallas import tpu as pltpu
from jax.sharding import PartitionSpec as P

ITERATIONS = 2
INTENSITY_FLOOR = 0.1
OBJECT_RATE = 0.05
PROBE_RATE = 0.5

CORES = 2
CHIPS_Z = 8
LANES = 128
MESH = pl.DeviceIdType.MESH
VMEM_LIMIT = 56 * 1024 * 1024


def dft_tables(length):
    index = np.arange(length // 2)
    scale = 1.0 / math.sqrt(length)
    tables = []
    for parity in range(2):
        phase = np.outer(index, 2 * index + parity) % length
        angle = phase * (-2.0 * math.pi / length)
        cosine, sine = np.cos(angle) * scale, np.sin(angle) * scale
        forward = np.block([[cosine, sine], [-sine, cosine]])
        for table in (forward, forward.T):
            high = table.astype(ml_dtypes.bfloat16)
            low = (table - high.astype(np.float64)).astype(ml_dtypes.bfloat16)
            tables += [high, low]
    order = np.concatenate([np.arange(0, length, 2), np.arange(1, length, 2)])
    tables.append(np.eye(length)[:, order].astype(ml_dtypes.bfloat16))
    return np.stack(tables)


def halves(values):
    high = values.astype(jnp.bfloat16)
    low = (values - high.astype(jnp.float32)).astype(jnp.bfloat16)
    return high, low


def product(left, right):
    dot = functools.partial(jnp.dot, preferred_element_type=jnp.float32)
    return dot(left[0], right[0]) + (dot(left[0], right[1]) + dot(left[1], right[0]))


def permuted(values, order):
    total = None
    for _ in range(3):
        part = values.astype(jnp.bfloat16)
        values = values - part.astype(jnp.float32)
        moved = jnp.dot(part, order, preferred_element_type=jnp.float32)
        total = moved if total is None else total + moved
    return total


def beside(parts):
    return jnp.concatenate(parts, axis=1)


def stacked(parts):
    return jnp.concatenate(parts, axis=0)


class Place:
    def __init__(self, chips_z):
        self.scan = lax.axis_index("scan")
        self.tile = lax.axis_index("tile")
        self.scans = lax.axis_size("scan")
        self.tiles = lax.axis_size("tile")
        self.chips_z = chips_z
        self.chips_x = self.scans // (chips_z * CORES)
        self.core = lax.rem(self.scan, CORES)
        self.z = lax.rem(self.scan // CORES, chips_z)
        self.x = self.scan // (CORES * chips_z)

    def at_core(self):
        return (self.scan + 1 - 2 * self.core, self.tile)

    def ring_x(self, k):
        x = lax.rem(self.x + k, self.chips_x)
        return x, ((x * self.chips_z + self.z) * CORES + self.core, self.tile)

    def ring_z(self, k):
        z = lax.rem(self.z + k, self.chips_z)
        return z, ((self.x * self.chips_z + z) * CORES + self.core, self.tile)

    def ring(self, axis, k):
        return self.ring_x(k) if axis == "x" else self.ring_tile(k)

    def along(self, axis):
        return (self.x, self.chips_x) if axis == "x" else (self.tile, self.tiles)

    def ring_tile(self, k):
        tile = lax.rem(self.tile + k, self.tiles)
        return tile, (self.scan, tile)

    def near(self, d):
        other = self.scan + d
        return jnp.logical_and(other >= 0, other < self.scans), (other, self.tile)


def distances(reach):
    far_first = sorted(range(1, reach + 1), reverse=True)
    return [sign * d for d in far_first for sign in (1, -1)]


def greet(partners):
    barrier = pltpu.get_barrier_semaphore()
    total = 0
    for condition, device in partners:
        if condition is None:
            pl.semaphore_signal(barrier, inc=1, device_id=device, device_id_type=MESH)
            total = total + 1
        else:

            @pl.when(condition)
            def _(device=device):
                pl.semaphore_signal(barrier, inc=1, device_id=device, device_id_type=MESH)

            total = total + condition.astype(jnp.int32)
    pl.semaphore_wait(barrier, total)


def sublane(shape):
    return lax.broadcasted_iota(jnp.int32, shape, 1)


def read_patch(band, row, patch):
    groups, margin = patch // 8, (band.shape[0] - patch) // 8
    tiled = band.reshape(groups + margin, 8, band.shape[1])
    block, inside = row // 8, lax.rem(row, 8)
    values = tiled[: groups + 1]
    for q in range(1, margin):
        values = jnp.where(block == q, tiled[q : q + groups + 1], values)
    turned = pltpu.roll(values, lax.rem(8 - inside, 8), 1)
    values = jnp.where(sublane(turned[1:].shape) < 8 - inside, turned[:-1], turned[1:])
    return values.reshape(patch, band.shape[1])


def place_patch(values, row, margin):
    patch, width = values.shape
    groups, margin = patch // 8, margin // 8
    block, inside = row // 8, lax.rem(row, 8)
    turned = pltpu.roll(values.reshape(groups, 8, width), inside, 1)
    edge = jnp.zeros((1, 8, width), values.dtype)
    before = stacked([edge, turned])
    after = stacked([turned, edge])
    values = jnp.where(sublane(before.shape) < inside, before, after)
    pad = jnp.zeros((margin - 1, 8, width), values.dtype)
    padded = stacked([pad, values, pad])
    band = padded[margin - 1 :]
    for q in range(1, margin):
        start = margin - 1 - q
        band = jnp.where(block == q, padded[start : start + groups + margin], band)
    return band.reshape((groups + margin) * 8, width)


def slot_gradient(row, window, modes, amplitude, tables, grad, grad_modes, patch_ref, pattern_ref, slot):
    patch = patch_ref.shape[1]
    count = modes.shape[0] // (2 * patch)
    half = patch // 2
    straight = [(tables[4 * p], tables[4 * p + 1]) for p in range(2)]
    turned = [(tables[4 * p + 2], tables[4 * p + 3]) for p in range(2)]

    def rows_of(part, m):
        return slice((part * count + m) * patch, (part * count + m + 1) * patch)

    for part in range(2):
        patch_ref[part] = read_patch(window[part], row, patch)
    pieces = [[], []]
    for m in range(count):
        patch_real, patch_imag = patch_ref[0], patch_ref[1]
        mode_real, mode_imag = modes[rows_of(0, m), :], modes[rows_of(1, m), :]
        real = mode_real * patch_real - mode_imag * patch_imag
        imag = mode_real * patch_imag + mode_imag * patch_real
        pieces[0].append(beside([real[:, :half] + real[:, half:], imag[:, :half] + imag[:, half:]]))
        pieces[1].append(beside([real[:, :half] - real[:, half:], imag[:, :half] - imag[:, half:]]))
    columns = [product(halves(stacked(pieces[p])), straight[p]) for p in range(2)]
    far = [[], []]
    power = [None, None]
    for m in range(count):
        even, odd = (columns[p][m * patch : (m + 1) * patch] for p in range(2))
        real = beside([even[:, :half], odd[:, :half]])
        imag = beside([even[:, half:], odd[:, half:]])
        pieces = (
            stacked([real[:half] + real[half:], imag[:half] + imag[half:]]),
            stacked([real[:half] - real[half:], imag[:half] - imag[half:]]),
        )
        for p in range(2):
            value = product(turned[p], halves(pieces[p]))
            far[p].append(value)
            square = value[:half] * value[:half] + value[half:] * value[half:]
            power[p] = square if power[p] is None else power[p] + square
    pattern = permuted(amplitude[...], tables[8])
    pattern_ref[0] = pattern[:, :half]
    pattern_ref[1] = pattern[:, half:]
    factor = []
    for p in range(2):
        pattern = beside([pattern_ref[q, pl.ds(p, half, stride=2), :] for q in range(2)])
        value = 1.0 - pattern * lax.rsqrt(jnp.maximum(power[p], INTENSITY_FLOOR))
        factor.append(stacked([value, value]))
    pieces = [[], []]
    for m in range(count):
        even, odd = (product(straight[p], halves(far[p][m] * factor[p])) for p in range(2))
        upper, lower = even + odd, even - odd
        real = stacked([upper[:half], lower[:half]])
        imag = stacked([upper[half:], lower[half:]])
        pieces[0].append(beside([real[:, :half], imag[:, :half]]))
        pieces[1].append(beside([real[:, half:], imag[:, half:]]))
    columns = [product(halves(stacked(pieces[p])), turned[p]) for p in range(2)]
    term_real = term_imag = None
    for m in range(count):
        even, odd = (columns[p][m * patch : (m + 1) * patch] for p in range(2))
        upper, lower = even + odd, even - odd
        back_real = beside([upper[:, :half], lower[:, :half]])
        back_imag = beside([upper[:, half:], lower[:, half:]])
        patch_real, patch_imag = patch_ref[0], patch_ref[1]
        mode_real, mode_imag = modes[rows_of(0, m), :], modes[rows_of(1, m), :]
        real = mode_real * back_real + mode_imag * back_imag
        imag = mode_real * back_imag - mode_imag * back_real
        term_real = real if term_real is None else term_real + real
        term_imag = imag if term_imag is None else term_imag + imag
        probe_real = patch_real * back_real + patch_imag * back_imag
        probe_imag = patch_real * back_imag - patch_imag * back_real
        if slot == 0:
            grad_modes[rows_of(0, m), :] = probe_real
            grad_modes[rows_of(1, m), :] = probe_imag
        else:
            grad_modes[rows_of(0, m), :] += probe_real
            grad_modes[rows_of(1, m), :] += probe_imag
    margin = window.shape[1] - patch
    grad[0] = place_patch(term_real, row, margin)
    grad[1] = place_patch(term_imag, row, margin)


def rows_at(start, size):
    return pl.ds(pl.multiple_of(start, 8), size)


def iterations_kernel(names, reach, chips_z, owners, rate, *refs):
    at_name = dict(zip(names, refs))
    first_field, first_modes = at_name["field"], at_name["modes"]
    rows_ref, amplitude, tables = at_name["rows"], at_name["amplitude"], at_name["tables"]
    columns, table = at_name["columns"], at_name["table"]
    place = Place(chips_z)
    _, rows, width = first_field.shape
    slots, patch = amplitude.shape[0], amplitude.shape[1]
    order = distances(reach)
    xs, ys, zs = place.chips_x, place.tiles, place.chips_z
    half = first_modes.shape[0] // CORES
    chains = (("x", "tile"), ("tile", "x"))
    chain = half // len(chains)
    part = chain // (xs * ys)
    piece = part // owners
    lane = lax.broadcasted_iota(jnp.int32, (rows, LANES), 1)
    blocks = width * ys // LANES
    wide = width // LANES
    finish = []

    def sems(name, *index):
        return at_name[name + "_send"].at[index], at_name[name + "_recv"].at[index]

    def copy_to(src, dst, device, name, *index):
        send, recv = sems(name, *index)
        return pltpu.make_async_remote_copy(
            src_ref=src, dst_ref=dst, send_sem=send, recv_sem=recv, device_id=device, device_id_type=MESH
        )

    def send(copy, condition=None):
        if condition is None:
            copy.start()
            finish.append(copy.wait_send)
        else:
            pl.when(condition)(copy.start)
            finish.append(lambda: pl.when(condition)(copy.wait_send))

    def owns(chain_at, z):
        return lax.rem(z + zs * len(chains) - chain_at * owners, zs)

    partners = [(None, place.at_core())]
    partners += [(None, place.ring_x(k)[1]) for k in range(1, xs)]
    partners += [(None, place.ring_tile(k)[1]) for k in range(1, ys)]
    for k in range(1, zs):
        z, device = place.ring_z(k)
        meets = functools.reduce(
            jnp.logical_or, [owns(c, at) < owners for c in range(len(chains)) for at in (z, place.z)]
        )
        partners.append((meets, device))
    partners += [place.near(d) for d in order]
    greet(partners)

    def share_strip(it, field):
        strip = at_name["strip"].at[it]
        own = pl.ds(pl.multiple_of(place.tile * width, LANES), width)
        copies = []
        for k in range(1, ys):
            copy = copy_to(field, strip.at[:, :, own], place.ring_tile(k)[1], "strip", it, k - 1)
            send(copy)
            copies.append(copy)
        strip[:, :, own] = field[...]
        return copies

    def cut(it, source, slot, target):
        strip = at_name["strip"].at[it]
        column = columns[source, 0, slot]
        first = column // LANES
        inside = column - first * LANES
        for p in range(2):
            pieces = []
            for i in range(wide + 1):
                value = strip[p, :, LANES * i : LANES * (i + 1)]
                for block in range(1, blocks - wide + 1):
                    at = min(block + i, blocks - 1)
                    value = jnp.where(first == block, strip[p, :, LANES * at : LANES * (at + 1)], value)
                pieces.append(pltpu.roll(value, lax.rem(LANES - inside, LANES), 1))
            for i in range(wide):
                target[p, :, LANES * i : LANES * (i + 1)] = jnp.where(
                    lane < LANES - inside, pieces[i], pieces[i + 1]
                )

    def send_windows(it, slot):
        window = at_name["window"].at[it, slot]
        copies = []
        for at, d in enumerate(order):
            exists, device = place.near(d)
            outgoing = at_name["outgoing"].at[it, slot, at]
            copy = copy_to(
                outgoing, window.at[:, (reach - d) * rows : (reach - d + 1) * rows, :],
                device, "window", it, slot, at,
            )
            cut(it, reach + d, slot, outgoing)
            send(copy, exists)
            copies.append((place.near(-d)[0], copy))
        cut(it, reach, slot, window.at[:, reach * rows : (reach + 1) * rows, :])
        return copies

    def send_gradient(it, slot):
        grad = at_name["grad"].at[it, slot]
        arrived = at_name["arrived"].at[it, slot]
        copies = []
        for at, d in enumerate(order):
            exists, device = place.near(d)
            copy = copy_to(
                grad.at[:, (reach + d) * rows : (reach + d + 1) * rows, :], arrived.at[reach - d],
                device, "grad", it, slot, at,
            )
            send(copy, exists)
            copies.append((place.near(-d)[0], copy))
        arrived[reach] = grad[:, reach * rows : (reach + 1) * rows, :]
        return copies

    def place_windows(it, slot):
        strip = at_name["grad_strip"].at[it]
        arrived = at_name["arrived"].at[it, slot]

        def place_window(source, carry):
            column = columns[source, 0, slot]
            first = column // LANES
            inside = column - first * LANES
            for p in range(2):
                values = [
                    pltpu.roll(arrived[source, p, :, LANES * i : LANES * (i + 1)], inside, 1)
                    for i in range(wide)
                ]
                values = [jnp.zeros_like(values[0])] + values + [jnp.zeros_like(values[0])]
                shifted = [jnp.where(lane < inside, values[i], values[i + 1]) for i in range(wide + 1)]
                for block in range(blocks):
                    term = jnp.zeros_like(values[0])
                    for i, value in enumerate(shifted):
                        term = jnp.where(first + i == block, value, term)
                    strip[p, :, LANES * block : LANES * (block + 1)] += term
            return carry

        lax.fori_loop(0, 2 * reach + 1, place_window, 0)

    def wait_near(copies):
        for exists, copy in copies:
            pl.when(exists)(copy.wait_recv)

    strip_copies = share_strip(0, first_field)
    table[reach] = at_name["own_columns"][...]
    notes = []
    for at, d in enumerate(order):
        exists, device = place.near(d)
        copy = copy_to(at_name["own_columns"], table.at[reach - d], device, "note", at)
        send(copy, exists)
        notes.append((place.near(-d)[0], copy))
    for d in order:

        @pl.when(jnp.logical_not(place.near(-d)[0]))
        def _(d=d):
            table[reach - d] = jnp.zeros(table.shape[1:], jnp.int32)
            for it in range(ITERATIONS):
                for slot in range(slots):
                    at_name["window"][it, slot, :, (reach - d) * rows : (reach - d + 1) * rows, :] = (
                        jnp.zeros((2, rows, patch), jnp.float32)
                    )
                    at_name["arrived"][it, slot, reach - d] = jnp.zeros((2, rows, patch), jnp.float32)

    at_name["grad_strip"][...] = jnp.zeros(at_name["grad_strip"].shape, jnp.float32)
    wait_near(notes)
    local = pltpu.make_async_copy(table, columns, at_name["local"])
    local.start()
    local.wait()
    for copy in strip_copies:
        copy.wait_recv()
    window_copies = [send_windows(0, slot) for slot in range(slots)]

    for it in range(ITERATIONS):
        last = it == ITERATIONS - 1
        field = first_field if it == 0 else at_name["field_between"]
        modes = first_modes if it == 0 else at_name["modes_between"]
        new_field = at_name["new_field"] if last else at_name["field_between"]
        new_modes = at_name["new_modes"] if last else at_name["modes_between"]
        grad_modes = at_name["grad_modes"].at[it]

        grad_copies = []
        for slot in range(slots):
            wait_near(window_copies[slot])
            slot_gradient(
                rows_ref[slot], at_name["window"].at[it, slot], modes, amplitude.at[slot], tables,
                at_name["grad"].at[it, slot], grad_modes, at_name["patch"], at_name["pattern"], slot,
            )
            if slot < slots - 1:
                grad_copies.append(send_gradient(it, slot))

        mine, other = place.core * half, (1 - place.core) * half
        core_part, core_sum = at_name["core_part"].at[it], at_name["core_sum"].at[it]
        core_copies = []
        for k in range(1, max(xs, ys) + 1):
            for c, (axis, _) in enumerate(chains):
                here, size = place.along(axis)
                if k > size:
                    continue
                quarter = chain // size
                start = c * chain + lax.rem(here + k, size) * quarter
                copy = copy_to(
                    grad_modes.at[rows_at(other + start, quarter)], core_part.at[rows_at(start, quarter)],
                    place.at_core(), "core", it, c, k - 1,
                )
                send(copy)
                core_copies.append((c, axis, k, size, quarter, start, copy))
        grad_copies.append(send_gradient(it, slots - 1))
        one_copies = [[], []]
        for c, axis, k, size, quarter, start, copy in core_copies:
            copy.wait_recv()
            at = rows_at(start, quarter)
            core_sum[at, :] = core_part[at, :] + grad_modes[rows_at(mine + start, quarter), :]
            if k < size:
                copy = copy_to(
                    core_sum.at[at], at_name["one_parts"].at[it, c, k - 1, pl.ds(0, quarter)],
                    place.ring(axis, k)[1], "one", it, c, k - 1,
                )
                send(copy)
                one_copies[c].append(copy)
        for slot in range(slots - 1):
            wait_near(grad_copies[slot])
            place_windows(it, slot)
        two_copies = [[], []]
        for c, (axis, axis_two) in enumerate(chains):
            here, size = place.along(axis)
            quarter = chain // size
            for copy in one_copies[c]:
                copy.wait_recv()
            total = core_sum[rows_at(c * chain + here * quarter, quarter), :]
            for k in range(size - 1):
                total = total + at_name["one_parts"][it, c, k, :quarter, :]
            one_sum = at_name["one_sum"].at[it, c, pl.ds(0, quarter)]
            one_sum[...] = total
            for k in range(1, place.along(axis_two)[1]):
                to, device = place.ring(axis_two, k)
                copy = copy_to(
                    one_sum.at[rows_at(to * part, part)], at_name["two_parts"].at[it, c, k - 1],
                    device, "two", it, c, k - 1,
                )
                send(copy)
                two_copies[c].append(copy)

        wait_near(grad_copies[slots - 1])
        place_windows(it, slots - 1)
        grad_strip = at_name["grad_strip"].at[it]
        tile_copies = []
        for k in range(1, ys):
            y, device = place.ring_tile(k)
            copy = copy_to(
                grad_strip.at[:, :, pl.ds(pl.multiple_of(y * width, LANES), width)],
                at_name["tile_parts"].at[it, k - 1], device, "tile", it, k - 1,
            )
            send(copy)
            tile_copies.append(copy)

        z_copies = [[], []]
        for c, (_, axis_two) in enumerate(chains):
            here, size = place.along(axis_two)
            for copy in two_copies[c]:
                copy.wait_recv()
            total = at_name["one_sum"][it, c, rows_at(here * part, part), :]
            for k in range(size - 1):
                total = total + at_name["two_parts"][it, c, k]
            two_sum = at_name["two_sum"].at[it, c]
            two_sum[...] = total
            for k in range(1, zs):
                z, device = place.ring_z(k)
                owned = owns(c, z)
                copy = copy_to(
                    two_sum.at[rows_at(jnp.minimum(owned, owners - 1) * piece, piece)],
                    at_name["z_parts"].at[it, c, k - 1], device, "z", it, c, k - 1,
                )
                send(copy, owned < owners)
                z_copies[c].append(copy)

        for copy in tile_copies:
            copy.wait_recv()
        total = grad_strip[:, :, pl.ds(pl.multiple_of(place.tile * width, LANES), width)]
        for k in range(ys - 1):
            total = total + at_name["tile_parts"][it, k]
        new_field[...] = field[...] - OBJECT_RATE * total
        if not last:
            strip_copies = share_strip(it + 1, new_field)

        my_quarters, my_parts, zg_copies = [], [], [[], []]
        for c, (axis, axis_two) in enumerate(chains):
            here, size = place.along(axis)
            my_quarter = mine + c * chain + here * (chain // size)
            my_part = my_quarter + place.along(axis_two)[0] * part
            my_quarters.append(my_quarter)
            my_parts.append(my_part)
            owned = owns(c, place.z)
            owner = owned < owners
            my_piece = jnp.minimum(owned, owners - 1) * piece

            @pl.when(owner)
            def _(c=c, my_part=my_part, my_piece=my_piece):
                for copy in z_copies[c]:
                    copy.wait_recv()
                total = at_name["two_sum"][it, c, rows_at(my_piece, piece), :]
                for k in range(zs - 1):
                    total = total + at_name["z_parts"][it, c, k]
                at = rows_at(my_part + my_piece, piece)
                new_modes[at, :] = modes[at, :] - rate * total

            for k in range(1, zs):
                ref = new_modes.at[rows_at(my_part + my_piece, piece)]
                copy = copy_to(ref, ref, place.ring_z(k)[1], "zg", it, c, k - 1)
                send(copy, owner)
                zg_copies[c].append((owns(c, lax.rem(place.z + zs - k, zs)) < owners, copy))
        two_copies = [[], []]
        for c, (_, axis_two) in enumerate(chains):
            wait_near(zg_copies[c])
            for k in range(1, place.along(axis_two)[1]):
                ref = new_modes.at[rows_at(my_parts[c], part)]
                copy = copy_to(ref, ref, place.ring(axis_two, k)[1], "twog", it, c, k - 1)
                send(copy)
                two_copies[c].append(copy)
        if not last:
            for copy in strip_copies:
                copy.wait_recv()
            window_copies = [send_windows(it + 1, slot) for slot in range(slots)]
        one_copies, core_copies = [[], []], []
        for c, (axis, _) in enumerate(chains):
            for copy in two_copies[c]:
                copy.wait_recv()
            here, size = place.along(axis)
            quarter = chain // size
            ref = new_modes.at[rows_at(my_quarters[c], quarter)]
            for k in range(1, size):
                copy = copy_to(ref, ref, place.ring(axis, k)[1], "oneg", it, c, k - 1)
                send(copy)
                one_copies[c].append(copy)
            copy = copy_to(ref, ref, place.at_core(), "coreg", it, c, 0)
            send(copy)
            core_copies.append(copy)
        for k in range(1, max(xs, ys)):
            for c, (axis, _) in enumerate(chains):
                here, size = place.along(axis)
                if k >= size:
                    continue
                one_copies[c][k - 1].wait_recv()
                quarter = chain // size
                start = mine + c * chain + lax.rem(here + size - k, size) * quarter
                ref = new_modes.at[rows_at(start, quarter)]
                copy = copy_to(ref, ref, place.at_core(), "coreg", it, c, k)
                send(copy)
                core_copies.append(copy)
        for copy in core_copies:
            copy.wait_recv()
    for wait in finish:
        wait()


def on_device(chips_z, object_field, probe, amplitude, positions, scan_list):
    _, rows, width = object_field.shape
    patch = probe.shape[2]
    reach = patch // (2 * rows)
    near = 2 * reach
    total = positions.shape[0]
    slots = scan_list.shape[0]
    tiles, scans = lax.axis_size("tile"), lax.axis_size("scan")
    chips_x = scans // (CORES * chips_z)
    flat = (probe.size // patch, patch)
    half = flat[0] // CORES
    chain = half // 2
    part = chain // (chips_x * tiles)
    owners = max(n for n in range(1, chips_z + 1) if part % (8 * n) == 0)
    piece = part // owners
    longest = max(chips_x, tiles)
    quarter = chain // min(chips_x, tiles)

    tables = jnp.asarray(dft_tables(patch))
    match = scan_list[:, None] == jnp.arange(total, dtype=jnp.int32)[None, :]
    found = jnp.sum(jnp.where(match[:, :, None], positions[None], 0), axis=1)
    row_start = found[:, 0] - lax.axis_index("scan") * rows + patch // 2
    own_columns = jnp.zeros((8, LANES), jnp.int32).at[0, :slots].set(found[:, 1])

    def vmem(*shape):
        return pltpu.VMEM((ITERATIONS,) + shape, jnp.float32)

    band = (2, (near + 1) * rows, patch)
    block = (2, rows, patch)
    scratch = {
        "columns": pltpu.SMEM((near + 1, 8, LANES), jnp.int32),
        "table": pltpu.VMEM((near + 1, 8, LANES), jnp.int32),
        "strip": vmem(2, rows, width * tiles),
        "outgoing": vmem(slots, near, *block),
        "window": vmem(slots, *band),
        "grad": vmem(slots, *band),
        "arrived": vmem(slots, near + 1, *block),
        "grad_strip": vmem(2, rows, width * tiles),
        "tile_parts": vmem(tiles - 1, 2, rows, width),
        "field_between": pltpu.VMEM(object_field.shape, jnp.float32),
        "modes_between": pltpu.VMEM(flat, jnp.float32),
        "patch": pltpu.VMEM((2, patch, patch), jnp.float32),
        "pattern": pltpu.VMEM((2, patch, patch // 2), jnp.float32),
        "grad_modes": vmem(*flat),
        "core_part": vmem(half, patch),
        "core_sum": vmem(half, patch),
        "one_parts": vmem(2, longest - 1, quarter, patch),
        "one_sum": vmem(2, quarter, patch),
        "two_parts": vmem(2, longest - 1, part, patch),
        "two_sum": vmem(2, part, patch),
        "z_parts": vmem(2, chips_z - 1, piece, patch),
        "local": pltpu.SemaphoreType.DMA(()),
    }
    counts = {
        "note": (near,),
        "strip": (ITERATIONS, tiles - 1),
        "window": (ITERATIONS, slots, near),
        "grad": (ITERATIONS, slots, near),
        "tile": (ITERATIONS, tiles - 1),
        "core": (ITERATIONS, 2, longest),
        "one": (ITERATIONS, 2, longest - 1),
        "two": (ITERATIONS, 2, longest - 1),
        "z": (ITERATIONS, 2, chips_z - 1),
        "zg": (ITERATIONS, 2, chips_z - 1),
        "twog": (ITERATIONS, 2, longest - 1),
        "oneg": (ITERATIONS, 2, longest - 1),
        "coreg": (ITERATIONS, 2, longest),
    }
    for name, shape in counts.items():
        scratch[name + "_send"] = pltpu.SemaphoreType.DMA(shape)
        scratch[name + "_recv"] = pltpu.SemaphoreType.DMA(shape)
    inputs = ["rows", "own_columns", "field", "modes", "amplitude", "tables"]
    outputs = ["new_field", "new_modes"]
    names = inputs + outputs + list(scratch)
    in_vmem = pl.BlockSpec(memory_space=pltpu.VMEM)
    field, modes = pl.pallas_call(
        functools.partial(iterations_kernel, names, reach, chips_z, owners, PROBE_RATE / total),
        out_shape=(
            jax.ShapeDtypeStruct(object_field.shape, jnp.float32),
            jax.ShapeDtypeStruct(flat, jnp.float32),
        ),
        in_specs=[pl.BlockSpec(memory_space=pltpu.SMEM)] + [in_vmem] * 5,
        out_specs=(in_vmem, in_vmem),
        scratch_shapes=list(scratch.values()),
        compiler_params=pltpu.CompilerParams(
            collective_id=1, has_side_effects=True, vmem_limit_bytes=VMEM_LIMIT
        ),
    )(row_start, own_columns, object_field, probe.reshape(flat), amplitude, tables)
    return field, modes.reshape(probe.shape)


def solution(mesh, chips_z=CHIPS_Z):
    in_specs = (
        P(None, "scan", "tile"),
        P(),
        P(("scan", "tile"), None, None),
        P(),
        P(("scan", "tile")),
    )
    out_specs = (P(None, "scan", "tile"), P())
    return jax.shard_map(
        functools.partial(on_device, chips_z),
        mesh=mesh,
        in_specs=in_specs,
        out_specs=out_specs,
        check_vma=False,
    )
```

```python
import functools
import math

import jax
import jax.numpy as jnp
import ml_dtypes
import numpy as np
from jax import lax
from jax.experimental import pallas as pl
from jax.experimental.pallas import tpu as pltpu
from jax.sharding import PartitionSpec as P

ITERATIONS = 2
INTENSITY_FLOOR = 0.1
OBJECT_RATE = 0.05
PROBE_RATE = 0.5

CORES = 2
CHIPS_Z = 8
LANES = 128
MESH = pl.DeviceIdType.MESH
STAGED = ("positions", "field", "modes", "amplitude", "tables")
VMEM_LIMIT = 56 * 1024 * 1024


def dft_tables(length):
    index = np.arange(length // 2)
    scale = 1.0 / math.sqrt(length)
    tables = []
    for parity in range(2):
        phase = np.outer(index, 2 * index + parity) % length
        angle = phase * (-2.0 * math.pi / length)
        cosine, sine = np.cos(angle) * scale, np.sin(angle) * scale
        forward = np.block([[cosine, sine], [-sine, cosine]])
        for table in (forward, forward.T):
            high = table.astype(ml_dtypes.bfloat16)
            low = (table - high.astype(np.float64)).astype(ml_dtypes.bfloat16)
            tables += [high, low]
    order = np.concatenate([np.arange(0, length, 2), np.arange(1, length, 2)])
    tables.append(np.eye(length)[:, order].astype(ml_dtypes.bfloat16))
    return np.stack(tables)


def halves(values):
    high = values.astype(jnp.bfloat16)
    low = (values - high.astype(jnp.float32)).astype(jnp.bfloat16)
    return high, low


def product(left, right):
    dot = functools.partial(jnp.dot, preferred_element_type=jnp.float32)
    return dot(left[0], right[0]) + (dot(left[0], right[1]) + dot(left[1], right[0]))


def permuted(values, order):
    total = None
    for _ in range(3):
        part = values.astype(jnp.bfloat16)
        values = values - part.astype(jnp.float32)
        moved = jnp.dot(part, order, preferred_element_type=jnp.float32)
        total = moved if total is None else total + moved
    return total


def beside(parts):
    return jnp.concatenate(parts, axis=1)


def stacked(parts):
    return jnp.concatenate(parts, axis=0)


class Place:
    def __init__(self, chips_z):
        self.scan = lax.axis_index("scan")
        self.tile = lax.axis_index("tile")
        self.scans = lax.axis_size("scan")
        self.tiles = lax.axis_size("tile")
        self.chips_z = chips_z
        self.chips_x = self.scans // (chips_z * CORES)
        self.core = lax.rem(self.scan, CORES)
        self.z = lax.rem(self.scan // CORES, chips_z)
        self.x = self.scan // (CORES * chips_z)

    def at_core(self):
        return (self.scan + 1 - 2 * self.core, self.tile)

    def ring_x(self, k):
        x = lax.rem(self.x + k, self.chips_x)
        return x, ((x * self.chips_z + self.z) * CORES + self.core, self.tile)

    def ring_z(self, k):
        z = lax.rem(self.z + k, self.chips_z)
        return z, ((self.x * self.chips_z + z) * CORES + self.core, self.tile)

    def ring(self, axis, k):
        return self.ring_x(k) if axis == "x" else self.ring_tile(k)

    def along(self, axis):
        return (self.x, self.chips_x) if axis == "x" else (self.tile, self.tiles)

    def ring_tile(self, k):
        tile = lax.rem(self.tile + k, self.tiles)
        return tile, (self.scan, tile)

    def near(self, d):
        other = self.scan + d
        return jnp.logical_and(other >= 0, other < self.scans), (other, self.tile)


def around(size):
    return sorted(range(1, size), key=lambda k: -min(k, size - k))


def distances(reach):
    far_first = sorted(range(1, reach + 1), reverse=True)
    return [sign * d for d in far_first for sign in (1, -1)]


def greet(partners):
    barrier = pltpu.get_barrier_semaphore()
    total = 0
    for condition, device in partners:
        if condition is None:
            pl.semaphore_signal(barrier, inc=1, device_id=device, device_id_type=MESH)
            total = total + 1
        else:

            @pl.when(condition)
            def _(device=device):
                pl.semaphore_signal(barrier, inc=1, device_id=device, device_id_type=MESH)

            total = total + condition.astype(jnp.int32)
    return lambda: pl.semaphore_wait(barrier, total)


def sublane(shape):
    return lax.broadcasted_iota(jnp.int32, shape, 1)


def read_patch(band, row, patch):
    groups, margin = patch // 8, (band.shape[0] - patch) // 8
    tiled = band.reshape(groups + margin, 8, band.shape[1])
    block, inside = row // 8, lax.rem(row, 8)
    values = tiled[: groups + 1]
    for q in range(1, margin):
        values = jnp.where(block == q, tiled[q : q + groups + 1], values)
    turned = pltpu.roll(values, lax.rem(8 - inside, 8), 1)
    values = jnp.where(sublane(turned[1:].shape) < 8 - inside, turned[:-1], turned[1:])
    return values.reshape(patch, band.shape[1])


def place_patch(values, row, margin):
    patch, width = values.shape
    groups, margin = patch // 8, margin // 8
    block, inside = row // 8, lax.rem(row, 8)
    turned = pltpu.roll(values.reshape(groups, 8, width), inside, 1)
    edge = jnp.zeros((1, 8, width), values.dtype)
    before = stacked([edge, turned])
    after = stacked([turned, edge])
    values = jnp.where(sublane(before.shape) < inside, before, after)
    pad = jnp.zeros((margin - 1, 8, width), values.dtype)
    padded = stacked([pad, values, pad])
    band = padded[margin - 1 :]
    for q in range(1, margin):
        start = margin - 1 - q
        band = jnp.where(block == q, padded[start : start + groups + margin], band)
    return band.reshape((groups + margin) * 8, width)


def slot_gradient(row, window, modes, amplitude, tables, grad, grad_modes, patch_ref, pattern_ref, slot):
    patch = patch_ref.shape[1]
    count = modes.shape[0] // (2 * patch)
    half = patch // 2
    straight = [(tables[4 * p], tables[4 * p + 1]) for p in range(2)]
    turned = [(tables[4 * p + 2], tables[4 * p + 3]) for p in range(2)]

    def rows_of(part, m):
        return slice((part * count + m) * patch, (part * count + m + 1) * patch)

    for part in range(2):
        patch_ref[part] = read_patch(window[part], row, patch)
    pieces = [[], []]
    for m in range(count):
        patch_real, patch_imag = patch_ref[0], patch_ref[1]
        mode_real, mode_imag = modes[rows_of(0, m), :], modes[rows_of(1, m), :]
        real = mode_real * patch_real - mode_imag * patch_imag
        imag = mode_real * patch_imag + mode_imag * patch_real
        pieces[0].append(beside([real[:, :half] + real[:, half:], imag[:, :half] + imag[:, half:]]))
        pieces[1].append(beside([real[:, :half] - real[:, half:], imag[:, :half] - imag[:, half:]]))
    columns = [product(halves(stacked(pieces[p])), straight[p]) for p in range(2)]
    far = [[], []]
    power = [None, None]
    for m in range(count):
        even, odd = (columns[p][m * patch : (m + 1) * patch] for p in range(2))
        real = beside([even[:, :half], odd[:, :half]])
        imag = beside([even[:, half:], odd[:, half:]])
        pieces = (
            stacked([real[:half] + real[half:], imag[:half] + imag[half:]]),
            stacked([real[:half] - real[half:], imag[:half] - imag[half:]]),
        )
        for p in range(2):
            value = product(turned[p], halves(pieces[p]))
            far[p].append(value)
            square = value[:half] * value[:half] + value[half:] * value[half:]
            power[p] = square if power[p] is None else power[p] + square
    pattern = permuted(amplitude[...], tables[8])
    pattern_ref[0] = pattern[:, :half]
    pattern_ref[1] = pattern[:, half:]
    factor = []
    for p in range(2):
        pattern = beside([pattern_ref[q, pl.ds(p, half, stride=2), :] for q in range(2)])
        value = 1.0 - pattern * lax.rsqrt(jnp.maximum(power[p], INTENSITY_FLOOR))
        factor.append(stacked([value, value]))
    pieces = [[], []]
    for m in range(count):
        even, odd = (product(straight[p], halves(far[p][m] * factor[p])) for p in range(2))
        upper, lower = even + odd, even - odd
        real = stacked([upper[:half], lower[:half]])
        imag = stacked([upper[half:], lower[half:]])
        pieces[0].append(beside([real[:, :half], imag[:, :half]]))
        pieces[1].append(beside([real[:, half:], imag[:, half:]]))
    columns = [product(halves(stacked(pieces[p])), turned[p]) for p in range(2)]
    term_real = term_imag = None
    for m in range(count):
        even, odd = (columns[p][m * patch : (m + 1) * patch] for p in range(2))
        upper, lower = even + odd, even - odd
        back_real = beside([upper[:, :half], lower[:, :half]])
        back_imag = beside([upper[:, half:], lower[:, half:]])
        patch_real, patch_imag = patch_ref[0], patch_ref[1]
        mode_real, mode_imag = modes[rows_of(0, m), :], modes[rows_of(1, m), :]
        real = mode_real * back_real + mode_imag * back_imag
        imag = mode_real * back_imag - mode_imag * back_real
        term_real = real if term_real is None else term_real + real
        term_imag = imag if term_imag is None else term_imag + imag
        probe_real = patch_real * back_real + patch_imag * back_imag
        probe_imag = patch_real * back_imag - patch_imag * back_real
        if slot == 0:
            grad_modes[rows_of(0, m), :] = probe_real
            grad_modes[rows_of(1, m), :] = probe_imag
        else:
            grad_modes[rows_of(0, m), :] += probe_real
            grad_modes[rows_of(1, m), :] += probe_imag
    margin = window.shape[1] - patch
    grad[0] = place_patch(term_real, row, margin)
    grad[1] = place_patch(term_imag, row, margin)


def rows_at(start, size):
    return pl.ds(pl.multiple_of(start, 8), size)


def iterations_kernel(names, reach, chips_z, owners, rate, *refs):
    at_name = dict(zip(names, refs))
    held = {name: at_name["held_" + name] for name in STAGED}
    first_field, first_modes = held["field"], held["modes"]
    amplitude, tables = held["amplitude"], held["tables"]
    notes_of, table = at_name["notes_of"], at_name["table"]
    place = Place(chips_z)
    _, rows, width = first_field.shape
    slots, patch = amplitude.shape[0], amplitude.shape[1]
    order = distances(reach)
    xs, ys, zs = place.chips_x, place.tiles, place.chips_z
    half = first_modes.shape[0] // CORES
    chains = (("x", "tile"), ("tile", "x"))
    chain = half // len(chains)
    part = chain // (xs * ys)
    piece = part // owners
    lane = lax.broadcasted_iota(jnp.int32, (rows, LANES), 1)
    blocks = width * ys // LANES
    wide = width // LANES
    finish = []

    def sems(name, *index):
        return at_name[name + "_send"].at[index], at_name[name + "_recv"].at[index]

    def copy_to(src, dst, device, name, *index):
        send, recv = sems(name, *index)
        return pltpu.make_async_remote_copy(
            src_ref=src, dst_ref=dst, send_sem=send, recv_sem=recv, device_id=device, device_id_type=MESH
        )

    def send(copy, condition=None):
        if condition is None:
            copy.start()
            finish.append(copy.wait_send)
        else:
            pl.when(condition)(copy.start)
            finish.append(lambda: pl.when(condition)(copy.wait_send))

    def owns(chain_at, z):
        return lax.rem(z + zs * len(chains) - chain_at * owners, zs)

    partners = [(None, place.at_core())]
    partners += [(None, place.ring_x(k)[1]) for k in range(1, xs)]
    partners += [(None, place.ring_tile(k)[1]) for k in range(1, ys)]
    for k in range(1, zs):
        z, device = place.ring_z(k)
        meets = functools.reduce(
            jnp.logical_or, [owns(c, at) < owners for c in range(len(chains)) for at in (z, place.z)]
        )
        partners.append((meets, device))
    partners += [place.near(d) for d in order]
    everyone_here = greet(partners)
    staged = {}
    for at, name in enumerate(STAGED):
        staged[name] = pltpu.make_async_copy(at_name[name], held[name], at_name["staged"].at[at])
        staged[name].start()

    def share_strip(it, field):
        strip = at_name["strip"].at[it]
        own = pl.ds(pl.multiple_of(place.tile * width, LANES), width)
        copies = []
        for k in around(ys):
            copy = copy_to(field, strip.at[:, :, own], place.ring_tile(k)[1], "strip", it, k - 1)
            send(copy)
            copies.append(copy)
        strip[:, :, own] = field[...]
        return copies

    def cut(it, source, slot, target):
        strip = at_name["strip"].at[it]
        column = notes_of[source, 1, slot]
        first = column // LANES
        inside = column - first * LANES
        for p in range(2):
            pieces = []
            for i in range(wide + 1):
                value = strip[p, :, LANES * i : LANES * (i + 1)]
                for block in range(1, blocks - wide + 1):
                    at = min(block + i, blocks - 1)
                    value = jnp.where(first == block, strip[p, :, LANES * at : LANES * (at + 1)], value)
                pieces.append(pltpu.roll(value, lax.rem(LANES - inside, LANES), 1))
            for i in range(wide):
                target[p, :, LANES * i : LANES * (i + 1)] = jnp.where(
                    lane < LANES - inside, pieces[i], pieces[i + 1]
                )

    def send_windows(it, slot):
        window = at_name["window"].at[it, slot]
        copies = []
        for at, d in enumerate(order):
            exists, device = place.near(d)
            outgoing = at_name["outgoing"].at[it, slot, at]
            copy = copy_to(
                outgoing, window.at[:, (reach - d) * rows : (reach - d + 1) * rows, :],
                device, "window", it, slot, at,
            )
            cut(it, reach + d, slot, outgoing)
            send(copy, exists)
            copies.append((place.near(-d)[0], copy))
        cut(it, reach, slot, window.at[:, reach * rows : (reach + 1) * rows, :])
        return copies

    def send_gradient(it, slot):
        grad = at_name["grad"].at[it, slot]
        arrived = at_name["arrived"].at[it, slot]
        copies = []
        for at, d in enumerate(order):
            exists, device = place.near(d)
            copy = copy_to(
                grad.at[:, (reach + d) * rows : (reach + d + 1) * rows, :], arrived.at[reach - d],
                device, "grad", it, slot, at,
            )
            send(copy, exists)
            copies.append((place.near(-d)[0], copy))
        arrived[reach] = grad[:, reach * rows : (reach + 1) * rows, :]
        return copies

    def place_windows(it, slot):
        strip = at_name["grad_strip"].at[it]
        arrived = at_name["arrived"].at[it, slot]

        def place_window(source, carry):
            column = notes_of[source, 1, slot]
            first = column // LANES
            inside = column - first * LANES
            for p in range(2):
                values = [
                    pltpu.roll(arrived[source, p, :, LANES * i : LANES * (i + 1)], inside, 1)
                    for i in range(wide)
                ]
                values = [jnp.zeros_like(values[0])] + values + [jnp.zeros_like(values[0])]
                shifted = [jnp.where(lane < inside, values[i], values[i + 1]) for i in range(wide + 1)]
                for block in range(blocks):
                    term = jnp.zeros_like(values[0])
                    for i, value in enumerate(shifted):
                        term = jnp.where(first + i == block, value, term)
                    strip[p, :, LANES * block : LANES * (block + 1)] += term
            return carry

        lax.fori_loop(0, 2 * reach + 1, place_window, 0)

    def wait_near(copies):
        for exists, copy in copies:
            pl.when(exists)(copy.wait_recv)

    for d in order:

        @pl.when(jnp.logical_not(place.near(-d)[0]))
        def _(d=d):
            table[reach - d] = jnp.zeros(table.shape[1:], jnp.int32)
            for it in range(ITERATIONS):
                for slot in range(slots):
                    at_name["window"][it, slot, :, (reach - d) * rows : (reach - d + 1) * rows, :] = (
                        jnp.zeros((2, rows, patch), jnp.float32)
                    )
                    at_name["arrived"][it, slot, reach - d] = jnp.zeros((2, rows, patch), jnp.float32)

    at_name["grad_strip"][...] = jnp.zeros(at_name["grad_strip"].shape, jnp.float32)
    staged["positions"].wait()
    position = held["positions"][...].astype(jnp.float32)
    index = lax.broadcasted_iota(jnp.int32, position.shape, 1)
    note_at = [lax.broadcasted_iota(jnp.int32, table.shape[1:], axis) for axis in range(2)]
    note = jnp.zeros(table.shape[1:], jnp.float32)
    for slot in range(slots):
        found = jnp.sum(jnp.where(index == at_name["scan_list"][slot], position, 0.0), axis=1, keepdims=True)
        for p in range(2):
            here = jnp.logical_and(note_at[0] == p, note_at[1] == slot)
            note = jnp.where(here, jnp.broadcast_to(found[p : p + 1], note.shape), note)
    table[reach] = note.astype(jnp.int32)
    staged["field"].wait()
    everyone_here()

    strip_copies = share_strip(0, first_field)
    notes = []
    for at, d in enumerate(order):
        exists, device = place.near(d)
        copy = copy_to(table.at[reach], table.at[reach - d], device, "note", at)
        send(copy, exists)
        notes.append((place.near(-d)[0], copy))
    wait_near(notes)
    local = pltpu.make_async_copy(table, notes_of, at_name["local"])
    local.start()
    local.wait()
    for copy in strip_copies:
        copy.wait_recv()
    window_copies = [send_windows(0, slot) for slot in range(slots)]
    for name in ("modes", "amplitude", "tables"):
        staged[name].wait()

    for it in range(ITERATIONS):
        last = it == ITERATIONS - 1
        field = first_field if it == 0 else at_name["field_between"]
        modes = first_modes if it == 0 else at_name["modes_between"]
        new_field = at_name["new_field"] if last else at_name["field_between"]
        new_modes = at_name["new_modes"] if last else at_name["modes_between"]
        grad_modes = at_name["grad_modes"].at[it]

        grad_copies = []
        for slot in range(slots):
            wait_near(window_copies[slot])
            slot_gradient(
                notes_of[reach, 0, slot] - place.scan * rows + patch // 2, at_name["window"].at[it, slot], modes, amplitude.at[slot], tables,
                at_name["grad"].at[it, slot], grad_modes, at_name["patch"], at_name["pattern"], slot,
            )
            if slot < slots - 1:
                grad_copies.append(send_gradient(it, slot))

        mine, other = place.core * half, (1 - place.core) * half
        core_part, core_sum = at_name["core_part"].at[it], at_name["core_sum"].at[it]
        core_copies = []
        for k in around(max(xs, ys)) + [max(xs, ys)]:
            for c, (axis, _) in enumerate(chains):
                here, size = place.along(axis)
                if k > size:
                    continue
                quarter = chain // size
                start = c * chain + lax.rem(here + k, size) * quarter
                copy = copy_to(
                    grad_modes.at[rows_at(other + start, quarter)], core_part.at[rows_at(start, quarter)],
                    place.at_core(), "core", it, c, k - 1,
                )
                send(copy)
                core_copies.append((c, axis, k, size, quarter, start, copy))
        grad_copies.append(send_gradient(it, slots - 1))
        one_copies = [[], []]
        for c, axis, k, size, quarter, start, copy in core_copies:
            copy.wait_recv()
            at = rows_at(start, quarter)
            core_sum[at, :] = core_part[at, :] + grad_modes[rows_at(mine + start, quarter), :]
            if k < size:
                copy = copy_to(
                    core_sum.at[at], at_name["one_parts"].at[it, c, k - 1, pl.ds(0, quarter)],
                    place.ring(axis, k)[1], "one", it, c, k - 1,
                )
                send(copy)
                one_copies[c].append(copy)
        if not last:
            for slot in range(slots - 1):
                wait_near(grad_copies[slot])
                place_windows(it, slot)
        two_copies = [[], []]
        for c, (axis, axis_two) in enumerate(chains):
            here, size = place.along(axis)
            quarter = chain // size
            for copy in one_copies[c]:
                copy.wait_recv()
            total = core_sum[rows_at(c * chain + here * quarter, quarter), :]
            for k in range(size - 1):
                total = total + at_name["one_parts"][it, c, k, :quarter, :]
            one_sum = at_name["one_sum"].at[it, c, pl.ds(0, quarter)]
            one_sum[...] = total
            for k in around(place.along(axis_two)[1]):
                to, device = place.ring(axis_two, k)
                copy = copy_to(
                    one_sum.at[rows_at(to * part, part)], at_name["two_parts"].at[it, c, k - 1],
                    device, "two", it, c, k - 1,
                )
                send(copy)
                two_copies[c].append(copy)

        grad_strip = at_name["grad_strip"].at[it]
        tile_copies = []

        def sum_windows(slot_range):
            for slot in slot_range:
                wait_near(grad_copies[slot])
                place_windows(it, slot)
            for k in around(ys):
                y, device = place.ring_tile(k)
                copy = copy_to(
                    grad_strip.at[:, :, pl.ds(pl.multiple_of(y * width, LANES), width)],
                    at_name["tile_parts"].at[it, k - 1], device, "tile", it, k - 1,
                )
                send(copy)
                tile_copies.append(copy)

        def update_field():
            for copy in tile_copies:
                copy.wait_recv()
            total = grad_strip[:, :, pl.ds(pl.multiple_of(place.tile * width, LANES), width)]
            for k in range(ys - 1):
                total = total + at_name["tile_parts"][it, k]
            new_field[...] = field[...] - OBJECT_RATE * total

        if not last:
            sum_windows(range(slots - 1, slots))
        z_copies = [[], []]
        for c, (_, axis_two) in enumerate(chains):
            here, size = place.along(axis_two)
            for copy in two_copies[c]:
                copy.wait_recv()
            total = at_name["one_sum"][it, c, rows_at(here * part, part), :]
            for k in range(size - 1):
                total = total + at_name["two_parts"][it, c, k]
            two_sum = at_name["two_sum"].at[it, c]
            two_sum[...] = total
            for k in around(zs):
                z, device = place.ring_z(k)
                owned = owns(c, z)
                copy = copy_to(
                    two_sum.at[rows_at(jnp.minimum(owned, owners - 1) * piece, piece)],
                    at_name["z_parts"].at[it, c, k - 1], device, "z", it, c, k - 1,
                )
                send(copy, owned < owners)
                z_copies[c].append(copy)

        if last:
            sum_windows(range(slots))
        else:
            update_field()
            strip_copies = share_strip(it + 1, new_field)

        my_quarters, my_parts, zg_copies = [], [], [[], []]
        for c, (axis, axis_two) in enumerate(chains):
            here, size = place.along(axis)
            my_quarter = mine + c * chain + here * (chain // size)
            my_part = my_quarter + place.along(axis_two)[0] * part
            my_quarters.append(my_quarter)
            my_parts.append(my_part)
            owned = owns(c, place.z)
            owner = owned < owners
            my_piece = jnp.minimum(owned, owners - 1) * piece

            @pl.when(owner)
            def _(c=c, my_part=my_part, my_piece=my_piece):
                for copy in z_copies[c]:
                    copy.wait_recv()
                total = at_name["two_sum"][it, c, rows_at(my_piece, piece), :]
                for k in range(zs - 1):
                    total = total + at_name["z_parts"][it, c, k]
                at = rows_at(my_part + my_piece, piece)
                new_modes[at, :] = modes[at, :] - rate * total

            for k in around(zs):
                ref = new_modes.at[rows_at(my_part + my_piece, piece)]
                copy = copy_to(ref, ref, place.ring_z(k)[1], "zg", it, c, k - 1)
                send(copy, owner)
                zg_copies[c].append((owns(c, lax.rem(place.z + zs - k, zs)) < owners, copy))
        two_copies = [[], []]
        for c, (_, axis_two) in enumerate(chains):
            wait_near(zg_copies[c])
            for k in around(place.along(axis_two)[1]):
                ref = new_modes.at[rows_at(my_parts[c], part)]
                copy = copy_to(ref, ref, place.ring(axis_two, k)[1], "twog", it, c, k - 1)
                send(copy)
                two_copies[c].append(copy)
        if last:
            update_field()
        else:
            for copy in strip_copies:
                copy.wait_recv()
            window_copies = [send_windows(it + 1, 0)]
        one_copies, core_copies = [{}, {}], []
        for c, (axis, _) in enumerate(chains):
            for copy in two_copies[c]:
                copy.wait_recv()
            here, size = place.along(axis)
            quarter = chain // size
            ref = new_modes.at[rows_at(my_quarters[c], quarter)]
            for k in around(size):
                copy = copy_to(ref, ref, place.ring(axis, k)[1], "oneg", it, c, k - 1)
                send(copy)
                one_copies[c][k] = copy
            copy = copy_to(ref, ref, place.at_core(), "coreg", it, c, 0)
            send(copy)
            core_copies.append(copy)
        if not last:
            window_copies += [send_windows(it + 1, slot) for slot in range(1, slots)]
        for k in around(max(xs, ys))[::-1]:
            for c, (axis, _) in enumerate(chains):
                here, size = place.along(axis)
                if k >= size:
                    continue
                one_copies[c][k].wait_recv()
                quarter = chain // size
                start = mine + c * chain + lax.rem(here + size - k, size) * quarter
                ref = new_modes.at[rows_at(start, quarter)]
                copy = copy_to(ref, ref, place.at_core(), "coreg", it, c, k)
                send(copy)
                core_copies.append(copy)
        for copy in core_copies:
            copy.wait_recv()
    for wait in finish:
        wait()


def hand_over_kernel(field_ref, modes_ref, field_out, modes_out, sems):
    copies = [
        pltpu.make_async_copy(field_ref, field_out, sems.at[0]),
        pltpu.make_async_copy(modes_ref, modes_out, sems.at[1]),
    ]
    for copy in copies:
        copy.start()
    for copy in copies:
        copy.wait()


def handed_over(field, modes):
    vmem, anywhere = pl.BlockSpec(memory_space=pltpu.VMEM), pl.BlockSpec(memory_space=pl.ANY)
    return pl.pallas_call(
        hand_over_kernel,
        out_shape=(
            jax.ShapeDtypeStruct(field.shape, jnp.float32),
            jax.ShapeDtypeStruct(modes.shape, jnp.float32),
        ),
        in_specs=[vmem, vmem],
        out_specs=(anywhere, anywhere),
        scratch_shapes=[pltpu.SemaphoreType.DMA((2,))],
    )(field, modes)


def on_device(chips_z, object_field, probe, amplitude, positions, scan_list):
    _, rows, width = object_field.shape
    patch = probe.shape[2]
    reach = patch // (2 * rows)
    near = 2 * reach
    total = positions.shape[0]
    slots = scan_list.shape[0]
    tiles, scans = lax.axis_size("tile"), lax.axis_size("scan")
    chips_x = scans // (CORES * chips_z)
    flat = (probe.size // patch, patch)
    half = flat[0] // CORES
    chain = half // 2
    part = chain // (chips_x * tiles)
    owners = max(n for n in range(1, chips_z + 1) if part % (8 * n) == 0)
    piece = part // owners
    longest = max(chips_x, tiles)
    quarter = chain // min(chips_x, tiles)

    tables = jnp.asarray(dft_tables(patch))

    def vmem(*shape):
        return pltpu.VMEM((ITERATIONS,) + shape, jnp.float32)

    band = (2, (near + 1) * rows, patch)
    block = (2, rows, patch)
    scratch = {
        "notes_of": pltpu.SMEM((near + 1, 8, LANES), jnp.int32),
        "table": pltpu.VMEM((near + 1, 8, LANES), jnp.int32),
        "strip": vmem(2, rows, width * tiles),
        "outgoing": vmem(slots, near, *block),
        "window": vmem(slots, *band),
        "grad": vmem(slots, *band),
        "arrived": vmem(slots, near + 1, *block),
        "grad_strip": vmem(2, rows, width * tiles),
        "tile_parts": vmem(tiles - 1, 2, rows, width),
        "field_between": pltpu.VMEM(object_field.shape, jnp.float32),
        "modes_between": pltpu.VMEM(flat, jnp.float32),
        "patch": pltpu.VMEM((2, patch, patch), jnp.float32),
        "pattern": pltpu.VMEM((2, patch, patch // 2), jnp.float32),
        "grad_modes": vmem(*flat),
        "core_part": vmem(half, patch),
        "core_sum": vmem(half, patch),
        "one_parts": vmem(2, longest - 1, quarter, patch),
        "one_sum": vmem(2, quarter, patch),
        "two_parts": vmem(2, longest - 1, part, patch),
        "two_sum": vmem(2, part, patch),
        "z_parts": vmem(2, chips_z - 1, piece, patch),
        "local": pltpu.SemaphoreType.DMA(()),
        "staged": pltpu.SemaphoreType.DMA((len(STAGED),)),
    }
    counts = {
        "note": (near,),
        "strip": (ITERATIONS, tiles - 1),
        "window": (ITERATIONS, slots, near),
        "grad": (ITERATIONS, slots, near),
        "tile": (ITERATIONS, tiles - 1),
        "core": (ITERATIONS, 2, longest),
        "one": (ITERATIONS, 2, longest - 1),
        "two": (ITERATIONS, 2, longest - 1),
        "z": (ITERATIONS, 2, chips_z - 1),
        "zg": (ITERATIONS, 2, chips_z - 1),
        "twog": (ITERATIONS, 2, longest - 1),
        "oneg": (ITERATIONS, 2, longest - 1),
        "coreg": (ITERATIONS, 2, longest),
    }
    for name, shape in counts.items():
        scratch[name + "_send"] = pltpu.SemaphoreType.DMA(shape)
        scratch[name + "_recv"] = pltpu.SemaphoreType.DMA(shape)
    operands = {
        "positions": positions.T,
        "field": object_field,
        "modes": probe.reshape(flat),
        "amplitude": amplitude,
        "tables": tables,
    }
    for name in STAGED:
        scratch["held_" + name] = pltpu.VMEM(operands[name].shape, operands[name].dtype)
    inputs = ["scan_list"] + list(STAGED)
    outputs = ["new_field", "new_modes"]
    names = inputs + outputs + list(scratch)
    in_vmem = pl.BlockSpec(memory_space=pltpu.VMEM)
    field, modes = pl.pallas_call(
        functools.partial(iterations_kernel, names, reach, chips_z, owners, PROBE_RATE / total),
        out_shape=(
            jax.ShapeDtypeStruct(object_field.shape, jnp.float32),
            jax.ShapeDtypeStruct(flat, jnp.float32),
        ),
        in_specs=[pl.BlockSpec(memory_space=pltpu.SMEM)]
        + [pl.BlockSpec(memory_space=pl.ANY)] * len(STAGED),
        out_specs=(in_vmem, in_vmem),
        scratch_shapes=list(scratch.values()),
        compiler_params=pltpu.CompilerParams(
            collective_id=1, has_side_effects=True, vmem_limit_bytes=VMEM_LIMIT
        ),
    )(scan_list, *[operands[name] for name in STAGED])
    field, modes = handed_over(field, modes)
    return field, modes.reshape(probe.shape)


def solution(mesh, chips_z=CHIPS_Z):
    in_specs = (
        P(None, "scan", "tile"),
        P(),
        P(("scan", "tile"), None, None),
        P(),
        P(("scan", "tile")),
    )
    out_specs = (P(None, "scan", "tile"), P())
    return jax.shard_map(
        functools.partial(on_device, chips_z),
        mesh=mesh,
        in_specs=in_specs,
        out_specs=out_specs,
        check_vma=False,
    )
```

```python
import functools
import math

import jax
import jax.numpy as jnp
import ml_dtypes
import numpy as np
from jax import lax
from jax.experimental import pallas as pl
from jax.experimental.pallas import tpu as pltpu
from jax.sharding import PartitionSpec as P

ITERATIONS = 2
INTENSITY_FLOOR = 0.1
OBJECT_RATE = 0.05
PROBE_RATE = 0.5

CORES = 2
CHIPS_Z = 8
LANES = 128
MESH = pl.DeviceIdType.MESH
STAGED = ("positions", "field", "modes", "amplitude", "tables")
VMEM_LIMIT = 56 * 1024 * 1024


def dft_tables(length):
    index = np.arange(length // 2)
    scale = 1.0 / math.sqrt(length)
    tables = []
    for parity in range(2):
        phase = np.outer(index, 2 * index + parity) % length
        angle = phase * (-2.0 * math.pi / length)
        cosine, sine = np.cos(angle) * scale, np.sin(angle) * scale
        forward = np.block([[cosine, sine], [-sine, cosine]])
        for table in (forward, forward.T):
            high = table.astype(ml_dtypes.bfloat16)
            low = (table - high.astype(np.float64)).astype(ml_dtypes.bfloat16)
            tables += [high, low]
    order = np.concatenate([np.arange(0, length, 2), np.arange(1, length, 2)])
    tables.append(np.eye(length)[:, order].astype(ml_dtypes.bfloat16))
    return np.stack(tables)


def halves(values):
    high = values.astype(jnp.bfloat16)
    low = (values - high.astype(jnp.float32)).astype(jnp.bfloat16)
    return high, low


def product(left, right):
    dot = functools.partial(jnp.dot, preferred_element_type=jnp.float32)
    return dot(left[0], right[0]) + (dot(left[0], right[1]) + dot(left[1], right[0]))


def permuted(values, order):
    total = None
    for _ in range(3):
        part = values.astype(jnp.bfloat16)
        values = values - part.astype(jnp.float32)
        moved = jnp.dot(part, order, preferred_element_type=jnp.float32)
        total = moved if total is None else total + moved
    return total


def beside(parts):
    return jnp.concatenate(parts, axis=1)


def stacked(parts):
    return jnp.concatenate(parts, axis=0)


class Place:
    def __init__(self, chips_z):
        self.scan = lax.axis_index("scan")
        self.tile = lax.axis_index("tile")
        self.scans = lax.axis_size("scan")
        self.tiles = lax.axis_size("tile")
        self.chips_z = chips_z
        self.chips_x = self.scans // (chips_z * CORES)
        self.core = lax.rem(self.scan, CORES)
        self.z = lax.rem(self.scan // CORES, chips_z)
        self.x = self.scan // (CORES * chips_z)

    def at_core(self):
        return (self.scan + 1 - 2 * self.core, self.tile)

    def ring_x(self, k):
        x = lax.rem(self.x + k, self.chips_x)
        return x, ((x * self.chips_z + self.z) * CORES + self.core, self.tile)

    def ring_z(self, k):
        z = lax.rem(self.z + k, self.chips_z)
        return z, ((self.x * self.chips_z + z) * CORES + self.core, self.tile)

    def ring(self, axis, k):
        return self.ring_x(k) if axis == "x" else self.ring_tile(k)

    def along(self, axis):
        return (self.x, self.chips_x) if axis == "x" else (self.tile, self.tiles)

    def ring_tile(self, k):
        tile = lax.rem(self.tile + k, self.tiles)
        return tile, (self.scan, tile)

    def near(self, d):
        other = self.scan + d
        return jnp.logical_and(other >= 0, other < self.scans), (other, self.tile)


def around(size):
    return sorted(range(1, size), key=lambda k: -min(k, size - k))


def distances(reach):
    far_first = sorted(range(1, reach + 1), reverse=True)
    return [sign * d for d in far_first for sign in (1, -1)]


def greet(partners):
    barrier = pltpu.get_barrier_semaphore()
    total = 0
    for condition, device in partners:
        if condition is None:
            pl.semaphore_signal(barrier, inc=1, device_id=device, device_id_type=MESH)
            total = total + 1
        else:

            @pl.when(condition)
            def _(device=device):
                pl.semaphore_signal(barrier, inc=1, device_id=device, device_id_type=MESH)

            total = total + condition.astype(jnp.int32)
    return lambda: pl.semaphore_wait(barrier, total)


def sublane(shape):
    return lax.broadcasted_iota(jnp.int32, shape, 1)


def read_patch(band, row, patch):
    groups, margin = patch // 8, (band.shape[0] - patch) // 8
    tiled = band.reshape(groups + margin, 8, band.shape[1])
    block, inside = row // 8, lax.rem(row, 8)
    values = tiled[: groups + 1]
    for q in range(1, margin):
        values = jnp.where(block == q, tiled[q : q + groups + 1], values)
    turned = pltpu.roll(values, lax.rem(8 - inside, 8), 1)
    values = jnp.where(sublane(turned[1:].shape) < 8 - inside, turned[:-1], turned[1:])
    return values.reshape(patch, band.shape[1])


def place_patch(values, row, margin):
    patch, width = values.shape
    groups, margin = patch // 8, margin // 8
    block, inside = row // 8, lax.rem(row, 8)
    turned = pltpu.roll(values.reshape(groups, 8, width), inside, 1)
    edge = jnp.zeros((1, 8, width), values.dtype)
    before = stacked([edge, turned])
    after = stacked([turned, edge])
    values = jnp.where(sublane(before.shape) < inside, before, after)
    pad = jnp.zeros((margin - 1, 8, width), values.dtype)
    padded = stacked([pad, values, pad])
    band = padded[margin - 1 :]
    for q in range(1, margin):
        start = margin - 1 - q
        band = jnp.where(block == q, padded[start : start + groups + margin], band)
    return band.reshape((groups + margin) * 8, width)


def slot_gradient(row, window, modes, patterns, tables, grad, grad_modes, patch_ref, slot):
    patch = patch_ref.shape[1]
    count = modes.shape[0] // (2 * patch)
    half = patch // 2
    straight = [(tables[4 * p], tables[4 * p + 1]) for p in range(2)]
    turned = [(tables[4 * p + 2], tables[4 * p + 3]) for p in range(2)]

    def rows_of(part, m):
        return slice((part * count + m) * patch, (part * count + m + 1) * patch)

    for part in range(2):
        patch_ref[part] = read_patch(window[part], row, patch)
    pieces = [[], []]
    for m in range(count):
        patch_real, patch_imag = patch_ref[0], patch_ref[1]
        mode_real, mode_imag = modes[rows_of(0, m), :], modes[rows_of(1, m), :]
        real = mode_real * patch_real - mode_imag * patch_imag
        imag = mode_real * patch_imag + mode_imag * patch_real
        pieces[0].append(beside([real[:, :half] + real[:, half:], imag[:, :half] + imag[:, half:]]))
        pieces[1].append(beside([real[:, :half] - real[:, half:], imag[:, :half] - imag[:, half:]]))
    columns = [product(halves(stacked(pieces[p])), straight[p]) for p in range(2)]
    far = [[], []]
    power = [None, None]
    for m in range(count):
        even, odd = (columns[p][m * patch : (m + 1) * patch] for p in range(2))
        real = beside([even[:, :half], odd[:, :half]])
        imag = beside([even[:, half:], odd[:, half:]])
        pieces = (
            stacked([real[:half] + real[half:], imag[:half] + imag[half:]]),
            stacked([real[:half] - real[half:], imag[:half] - imag[half:]]),
        )
        for p in range(2):
            value = product(turned[p], halves(pieces[p]))
            far[p].append(value)
            square = value[:half] * value[:half] + value[half:] * value[half:]
            power[p] = square if power[p] is None else power[p] + square
    factor = []
    for p in range(2):
        value = 1.0 - patterns[p] * lax.rsqrt(jnp.maximum(power[p], INTENSITY_FLOOR))
        factor.append(stacked([value, value]))
    pieces = [[], []]
    for m in range(count):
        even, odd = (product(straight[p], halves(far[p][m] * factor[p])) for p in range(2))
        upper, lower = even + odd, even - odd
        real = stacked([upper[:half], lower[:half]])
        imag = stacked([upper[half:], lower[half:]])
        pieces[0].append(beside([real[:, :half], imag[:, :half]]))
        pieces[1].append(beside([real[:, half:], imag[:, half:]]))
    columns = [product(halves(stacked(pieces[p])), turned[p]) for p in range(2)]
    term_real = term_imag = None
    for m in range(count):
        even, odd = (columns[p][m * patch : (m + 1) * patch] for p in range(2))
        upper, lower = even + odd, even - odd
        back_real = beside([upper[:, :half], lower[:, :half]])
        back_imag = beside([upper[:, half:], lower[:, half:]])
        patch_real, patch_imag = patch_ref[0], patch_ref[1]
        mode_real, mode_imag = modes[rows_of(0, m), :], modes[rows_of(1, m), :]
        real = mode_real * back_real + mode_imag * back_imag
        imag = mode_real * back_imag - mode_imag * back_real
        term_real = real if term_real is None else term_real + real
        term_imag = imag if term_imag is None else term_imag + imag
        probe_real = patch_real * back_real + patch_imag * back_imag
        probe_imag = patch_real * back_imag - patch_imag * back_real
        if slot == 0:
            grad_modes[rows_of(0, m), :] = probe_real
            grad_modes[rows_of(1, m), :] = probe_imag
        else:
            grad_modes[rows_of(0, m), :] += probe_real
            grad_modes[rows_of(1, m), :] += probe_imag
    margin = window.shape[1] - patch
    grad[0] = place_patch(term_real, row, margin)
    grad[1] = place_patch(term_imag, row, margin)


def rows_at(start, size):
    return pl.ds(pl.multiple_of(start, 8), size)


def iterations_kernel(names, reach, chips_z, owners, rate, *refs):
    at_name = dict(zip(names, refs))
    held = {name: at_name["held_" + name] for name in STAGED}
    first_field, first_modes = held["field"], held["modes"]
    amplitude, tables = held["amplitude"], held["tables"]
    notes_of, table = at_name["notes_of"], at_name["table"]
    place = Place(chips_z)
    _, rows, width = first_field.shape
    slots, patch = amplitude.shape[0], amplitude.shape[1]
    order = distances(reach)
    xs, ys, zs = place.chips_x, place.tiles, place.chips_z
    half = first_modes.shape[0] // CORES
    chains = (("x", "tile"), ("tile", "x"))
    chain = half // len(chains)
    part = chain // (xs * ys)
    piece = part // owners
    lane = lax.broadcasted_iota(jnp.int32, (rows, LANES), 1)
    blocks = width * ys // LANES
    wide = width // LANES
    finish = []

    def sems(name, *index):
        return at_name[name + "_send"].at[index], at_name[name + "_recv"].at[index]

    def copy_to(src, dst, device, name, *index):
        send, recv = sems(name, *index)
        return pltpu.make_async_remote_copy(
            src_ref=src, dst_ref=dst, send_sem=send, recv_sem=recv, device_id=device, device_id_type=MESH
        )

    def send(copy, condition=None):
        if condition is None:
            copy.start()
            finish.append(copy.wait_send)
        else:
            pl.when(condition)(copy.start)
            finish.append(lambda: pl.when(condition)(copy.wait_send))

    def owns(chain_at, z):
        return lax.rem(z + zs * len(chains) - chain_at * owners, zs)

    partners = [(None, place.at_core())]
    partners += [(None, place.ring_x(k)[1]) for k in range(1, xs)]
    partners += [(None, place.ring_tile(k)[1]) for k in range(1, ys)]
    for k in range(1, zs):
        z, device = place.ring_z(k)
        meets = functools.reduce(
            jnp.logical_or, [owns(c, at) < owners for c in range(len(chains)) for at in (z, place.z)]
        )
        partners.append((meets, device))
    partners += [place.near(d) for d in order]
    everyone_here = greet(partners)
    staged = {}
    for at, name in enumerate(STAGED):
        staged[name] = pltpu.make_async_copy(at_name[name], held[name], at_name["staged"].at[at])
        staged[name].start()

    def share_strip(it, field):
        strip = at_name["strip"].at[it]
        own = pl.ds(pl.multiple_of(place.tile * width, LANES), width)
        copies = []
        for k in around(ys):
            copy = copy_to(field, strip.at[:, :, own], place.ring_tile(k)[1], "strip", it, k - 1)
            send(copy)
            copies.append(copy)
        strip[:, :, own] = field[...]
        return copies

    def cut(it, source, slot, target):
        strip = at_name["strip"].at[it]
        column = notes_of[source, 1, slot]
        first = column // LANES
        inside = column - first * LANES
        for p in range(2):
            pieces = []
            for i in range(wide + 1):
                value = strip[p, :, LANES * i : LANES * (i + 1)]
                for block in range(1, blocks - wide + 1):
                    at = min(block + i, blocks - 1)
                    value = jnp.where(first == block, strip[p, :, LANES * at : LANES * (at + 1)], value)
                pieces.append(pltpu.roll(value, lax.rem(LANES - inside, LANES), 1))
            for i in range(wide):
                target[p, :, LANES * i : LANES * (i + 1)] = jnp.where(
                    lane < LANES - inside, pieces[i], pieces[i + 1]
                )

    def send_windows(it, slot):
        window = at_name["window"].at[it, slot]
        copies = []
        for at, d in enumerate(order):
            exists, device = place.near(d)
            outgoing = at_name["outgoing"].at[it, slot, at]
            copy = copy_to(
                outgoing, window.at[:, (reach - d) * rows : (reach - d + 1) * rows, :],
                device, "window", it, slot, at,
            )
            cut(it, reach + d, slot, outgoing)
            send(copy, exists)
            copies.append((place.near(-d)[0], copy))
        cut(it, reach, slot, window.at[:, reach * rows : (reach + 1) * rows, :])
        return copies

    def send_gradient(it, slot):
        grad = at_name["grad"].at[it, slot]
        arrived = at_name["arrived"].at[it, slot]
        copies = []
        for at, d in enumerate(order):
            exists, device = place.near(d)
            copy = copy_to(
                grad.at[:, (reach + d) * rows : (reach + d + 1) * rows, :], arrived.at[reach - d],
                device, "grad", it, slot, at,
            )
            send(copy, exists)
            copies.append((place.near(-d)[0], copy))
        arrived[reach] = grad[:, reach * rows : (reach + 1) * rows, :]
        return copies

    def place_windows(it, slot):
        strip = at_name["grad_strip"].at[it]
        arrived = at_name["arrived"].at[it, slot]

        def place_window(source, carry):
            column = notes_of[source, 1, slot]
            first = column // LANES
            inside = column - first * LANES
            for p in range(2):
                values = [
                    pltpu.roll(arrived[source, p, :, LANES * i : LANES * (i + 1)], inside, 1)
                    for i in range(wide)
                ]
                values = [jnp.zeros_like(values[0])] + values + [jnp.zeros_like(values[0])]
                shifted = [jnp.where(lane < inside, values[i], values[i + 1]) for i in range(wide + 1)]
                for block in range(blocks):
                    term = jnp.zeros_like(values[0])
                    for i, value in enumerate(shifted):
                        term = jnp.where(first + i == block, value, term)
                    strip[p, :, LANES * block : LANES * (block + 1)] += term
            return carry

        lax.fori_loop(0, 2 * reach + 1, place_window, 0)

    def wait_near(copies):
        for exists, copy in copies:
            pl.when(exists)(copy.wait_recv)

    for d in order:

        @pl.when(jnp.logical_not(place.near(-d)[0]))
        def _(d=d):
            table[reach - d] = jnp.zeros(table.shape[1:], jnp.int32)
            for it in range(ITERATIONS):
                for slot in range(slots):
                    at_name["window"][it, slot, :, (reach - d) * rows : (reach - d + 1) * rows, :] = (
                        jnp.zeros((2, rows, patch), jnp.float32)
                    )
                    at_name["arrived"][it, slot, reach - d] = jnp.zeros((2, rows, patch), jnp.float32)

    at_name["grad_strip"][...] = jnp.zeros(at_name["grad_strip"].shape, jnp.float32)
    staged["positions"].wait()
    position = held["positions"][...].astype(jnp.float32)
    index = lax.broadcasted_iota(jnp.int32, position.shape, 1)
    note_at = [lax.broadcasted_iota(jnp.int32, table.shape[1:], axis) for axis in range(2)]
    note = jnp.zeros(table.shape[1:], jnp.float32)
    for slot in range(slots):
        found = jnp.sum(jnp.where(index == at_name["scan_list"][slot], position, 0.0), axis=1, keepdims=True)
        for p in range(2):
            here = jnp.logical_and(note_at[0] == p, note_at[1] == slot)
            note = jnp.where(here, jnp.broadcast_to(found[p : p + 1], note.shape), note)
    table[reach] = note.astype(jnp.int32)
    staged["field"].wait()
    everyone_here()

    strip_copies = share_strip(0, first_field)
    notes = []
    for at, d in enumerate(order):
        exists, device = place.near(d)
        copy = copy_to(table.at[reach], table.at[reach - d], device, "note", at)
        send(copy, exists)
        notes.append((place.near(-d)[0], copy))
    wait_near(notes)
    local = pltpu.make_async_copy(table, notes_of, at_name["local"])
    local.start()
    local.wait()
    for copy in strip_copies:
        copy.wait_recv()
    window_copies = [send_windows(0, slot) for slot in range(slots)]
    for name in ("modes", "amplitude", "tables"):
        staged[name].wait()
    for slot in range(slots):
        pattern = permuted(amplitude[slot], tables[8])
        for q in range(2):
            at_name["pattern"][slot, q] = pattern[:, q * (patch // 2) : (q + 1) * (patch // 2)]
        for p in range(2):
            at_name["patterns"][slot, p] = beside(
                [at_name["pattern"][slot, q, pl.ds(p, patch // 2, stride=2), :] for q in range(2)]
            )

    for it in range(ITERATIONS):
        last = it == ITERATIONS - 1
        field = first_field if it == 0 else at_name["field_between"]
        modes = first_modes if it == 0 else at_name["modes_between"]
        new_field = at_name["new_field"] if last else at_name["field_between"]
        new_modes = at_name["new_modes"] if last else at_name["modes_between"]
        grad_modes = at_name["grad_modes"].at[it]

        grad_copies = []
        for slot in range(slots):
            wait_near(window_copies[slot])
            slot_gradient(
                notes_of[reach, 0, slot] - place.scan * rows + patch // 2, at_name["window"].at[it, slot], modes, at_name["patterns"].at[slot], tables,
                at_name["grad"].at[it, slot], grad_modes, at_name["patch"], slot,
            )
            if slot < slots - 1:
                grad_copies.append(send_gradient(it, slot))

        mine, other = place.core * half, (1 - place.core) * half
        core_part, core_sum = at_name["core_part"].at[it], at_name["core_sum"].at[it]
        core_copies = []
        for k in around(max(xs, ys)) + [max(xs, ys)]:
            for c, (axis, _) in enumerate(chains):
                here, size = place.along(axis)
                if k > size:
                    continue
                quarter = chain // size
                start = c * chain + lax.rem(here + k, size) * quarter
                copy = copy_to(
                    grad_modes.at[rows_at(other + start, quarter)], core_part.at[rows_at(start, quarter)],
                    place.at_core(), "core", it, c, k - 1,
                )
                send(copy)
                core_copies.append((c, axis, k, size, quarter, start, copy))
        grad_copies.append(send_gradient(it, slots - 1))
        one_copies = [[], []]
        for c, axis, k, size, quarter, start, copy in core_copies:
            copy.wait_recv()
            at = rows_at(start, quarter)
            core_sum[at, :] = core_part[at, :] + grad_modes[rows_at(mine + start, quarter), :]
            if k < size:
                copy = copy_to(
                    core_sum.at[at], at_name["one_parts"].at[it, c, k - 1, pl.ds(0, quarter)],
                    place.ring(axis, k)[1], "one", it, c, k - 1,
                )
                send(copy)
                one_copies[c].append(copy)
        if not last:
            for slot in range(slots - 1):
                wait_near(grad_copies[slot])
                place_windows(it, slot)
        two_copies = [[], []]
        for c, (axis, axis_two) in enumerate(chains):
            here, size = place.along(axis)
            quarter = chain // size
            for copy in one_copies[c]:
                copy.wait_recv()
            total = core_sum[rows_at(c * chain + here * quarter, quarter), :]
            for k in range(size - 1):
                total = total + at_name["one_parts"][it, c, k, :quarter, :]
            one_sum = at_name["one_sum"].at[it, c, pl.ds(0, quarter)]
            one_sum[...] = total
            for k in around(place.along(axis_two)[1]):
                to, device = place.ring(axis_two, k)
                copy = copy_to(
                    one_sum.at[rows_at(to * part, part)], at_name["two_parts"].at[it, c, k - 1],
                    device, "two", it, c, k - 1,
                )
                send(copy)
                two_copies[c].append(copy)

        grad_strip = at_name["grad_strip"].at[it]
        tile_copies = []

        def sum_windows(slot_range):
            for slot in slot_range:
                wait_near(grad_copies[slot])
                place_windows(it, slot)
            for k in around(ys):
                y, device = place.ring_tile(k)
                copy = copy_to(
                    grad_strip.at[:, :, pl.ds(pl.multiple_of(y * width, LANES), width)],
                    at_name["tile_parts"].at[it, k - 1], device, "tile", it, k - 1,
                )
                send(copy)
                tile_copies.append(copy)

        def update_field():
            for copy in tile_copies:
                copy.wait_recv()
            total = grad_strip[:, :, pl.ds(pl.multiple_of(place.tile * width, LANES), width)]
            for k in range(ys - 1):
                total = total + at_name["tile_parts"][it, k]
            new_field[...] = field[...] - OBJECT_RATE * total

        if not last:
            sum_windows(range(slots - 1, slots))
        z_copies = [[], []]
        for c, (_, axis_two) in enumerate(chains):
            here, size = place.along(axis_two)
            for copy in two_copies[c]:
                copy.wait_recv()
            total = at_name["one_sum"][it, c, rows_at(here * part, part), :]
            for k in range(size - 1):
                total = total + at_name["two_parts"][it, c, k]
            two_sum = at_name["two_sum"].at[it, c]
            two_sum[...] = total
            for k in around(zs):
                z, device = place.ring_z(k)
                owned = owns(c, z)
                copy = copy_to(
                    two_sum.at[rows_at(jnp.minimum(owned, owners - 1) * piece, piece)],
                    at_name["z_parts"].at[it, c, k - 1], device, "z", it, c, k - 1,
                )
                send(copy, owned < owners)
                z_copies[c].append(copy)

        if last:
            sum_windows(range(slots))
        else:
            update_field()
            strip_copies = share_strip(it + 1, new_field)

        my_quarters, my_parts, zg_copies = [], [], [[], []]
        for c, (axis, axis_two) in enumerate(chains):
            here, size = place.along(axis)
            my_quarter = mine + c * chain + here * (chain // size)
            my_part = my_quarter + place.along(axis_two)[0] * part
            my_quarters.append(my_quarter)
            my_parts.append(my_part)
            owned = owns(c, place.z)
            owner = owned < owners
            my_piece = jnp.minimum(owned, owners - 1) * piece

            @pl.when(owner)
            def _(c=c, my_part=my_part, my_piece=my_piece):
                for copy in z_copies[c]:
                    copy.wait_recv()
                total = at_name["two_sum"][it, c, rows_at(my_piece, piece), :]
                for k in range(zs - 1):
                    total = total + at_name["z_parts"][it, c, k]
                at = rows_at(my_part + my_piece, piece)
                new_modes[at, :] = modes[at, :] - rate * total

            for k in around(zs):
                ref = new_modes.at[rows_at(my_part + my_piece, piece)]
                copy = copy_to(ref, ref, place.ring_z(k)[1], "zg", it, c, k - 1)
                send(copy, owner)
                zg_copies[c].append((owns(c, lax.rem(place.z + zs - k, zs)) < owners, copy))
        two_copies = [[], []]
        one_copies, core_copies = [{}, {}], []

        def pass_on(c, which, start):
            axis = chains[c][0]
            ref = new_modes.at[rows_at(start, part)]
            for k in around(place.along(axis)[1]):
                copy = copy_to(ref, ref, place.ring(axis, k)[1], "oneg", it, c, k - 1, which)
                send(copy)
                one_copies[c][k, which] = copy

        for c, (_, axis_two) in enumerate(chains):
            wait_near(zg_copies[c])
            for k in around(place.along(axis_two)[1]):
                ref = new_modes.at[rows_at(my_parts[c], part)]
                copy = copy_to(ref, ref, place.ring(axis_two, k)[1], "twog", it, c, k - 1)
                send(copy)
                two_copies[c].append((k, copy))
            pass_on(c, 0, my_parts[c])
        if last:
            update_field()
        else:
            for copy in strip_copies:
                copy.wait_recv()
            window_copies = [send_windows(it + 1, 0)]
        for c, (axis, axis_two) in enumerate(chains):
            here_two, size_two = place.along(axis_two)
            for k, copy in reversed(two_copies[c]):
                copy.wait_recv()
                pass_on(c, k, my_quarters[c] + lax.rem(here_two + size_two - k, size_two) * part)
            here, size = place.along(axis)
            quarter = chain // size
            ref = new_modes.at[rows_at(my_quarters[c], quarter)]
            copy = copy_to(ref, ref, place.at_core(), "coreg", it, c, 0)
            send(copy)
            core_copies.append(copy)
        if not last:
            window_copies += [send_windows(it + 1, slot) for slot in range(1, slots)]
        for k in around(max(xs, ys))[::-1]:
            for c, (axis, _) in enumerate(chains):
                here, size = place.along(axis)
                if k >= size:
                    continue
                for which in range(place.along(chains[c][1])[1]):
                    one_copies[c][k, which].wait_recv()
                quarter = chain // size
                start = mine + c * chain + lax.rem(here + size - k, size) * quarter
                ref = new_modes.at[rows_at(start, quarter)]
                copy = copy_to(ref, ref, place.at_core(), "coreg", it, c, k)
                send(copy)
                core_copies.append(copy)
        for copy in core_copies:
            copy.wait_recv()
    for wait in finish:
        wait()


def hand_over_kernel(field_ref, modes_ref, field_out, modes_out, sems):
    copies = [
        pltpu.make_async_copy(field_ref, field_out, sems.at[0]),
        pltpu.make_async_copy(modes_ref, modes_out, sems.at[1]),
    ]
    for copy in copies:
        copy.start()
    for copy in copies:
        copy.wait()


def handed_over(field, modes):
    vmem, anywhere = pl.BlockSpec(memory_space=pltpu.VMEM), pl.BlockSpec(memory_space=pl.ANY)
    return pl.pallas_call(
        hand_over_kernel,
        out_shape=(
            jax.ShapeDtypeStruct(field.shape, jnp.float32),
            jax.ShapeDtypeStruct(modes.shape, jnp.float32),
        ),
        in_specs=[vmem, vmem],
        out_specs=(anywhere, anywhere),
        scratch_shapes=[pltpu.SemaphoreType.DMA((2,))],
    )(field, modes)


def on_device(chips_z, object_field, probe, amplitude, positions, scan_list):
    _, rows, width = object_field.shape
    patch = probe.shape[2]
    reach = patch // (2 * rows)
    near = 2 * reach
    total = positions.shape[0]
    slots = scan_list.shape[0]
    tiles, scans = lax.axis_size("tile"), lax.axis_size("scan")
    chips_x = scans // (CORES * chips_z)
    flat = (probe.size // patch, patch)
    half = flat[0] // CORES
    chain = half // 2
    part = chain // (chips_x * tiles)
    owners = max(n for n in range(1, chips_z + 1) if part % (8 * n) == 0)
    piece = part // owners
    longest = max(chips_x, tiles)
    quarter = chain // min(chips_x, tiles)

    tables = jnp.asarray(dft_tables(patch))

    def vmem(*shape):
        return pltpu.VMEM((ITERATIONS,) + shape, jnp.float32)

    band = (2, (near + 1) * rows, patch)
    block = (2, rows, patch)
    scratch = {
        "notes_of": pltpu.SMEM((near + 1, 8, LANES), jnp.int32),
        "table": pltpu.VMEM((near + 1, 8, LANES), jnp.int32),
        "strip": vmem(2, rows, width * tiles),
        "outgoing": vmem(slots, near, *block),
        "window": vmem(slots, *band),
        "grad": vmem(slots, *band),
        "arrived": vmem(slots, near + 1, *block),
        "grad_strip": vmem(2, rows, width * tiles),
        "tile_parts": vmem(tiles - 1, 2, rows, width),
        "field_between": pltpu.VMEM(object_field.shape, jnp.float32),
        "modes_between": pltpu.VMEM(flat, jnp.float32),
        "patch": pltpu.VMEM((2, patch, patch), jnp.float32),
        "pattern": pltpu.VMEM((slots, 2, patch, patch // 2), jnp.float32),
        "patterns": pltpu.VMEM((slots, 2, patch // 2, patch), jnp.float32),
        "grad_modes": vmem(*flat),
        "core_part": vmem(half, patch),
        "core_sum": vmem(half, patch),
        "one_parts": vmem(2, longest - 1, quarter, patch),
        "one_sum": vmem(2, quarter, patch),
        "two_parts": vmem(2, longest - 1, part, patch),
        "two_sum": vmem(2, part, patch),
        "z_parts": vmem(2, chips_z - 1, piece, patch),
        "local": pltpu.SemaphoreType.DMA(()),
        "staged": pltpu.SemaphoreType.DMA((len(STAGED),)),
    }
    counts = {
        "note": (near,),
        "strip": (ITERATIONS, tiles - 1),
        "window": (ITERATIONS, slots, near),
        "grad": (ITERATIONS, slots, near),
        "tile": (ITERATIONS, tiles - 1),
        "core": (ITERATIONS, 2, longest),
        "one": (ITERATIONS, 2, longest - 1),
        "two": (ITERATIONS, 2, longest - 1),
        "z": (ITERATIONS, 2, chips_z - 1),
        "zg": (ITERATIONS, 2, chips_z - 1),
        "twog": (ITERATIONS, 2, longest - 1),
        "oneg": (ITERATIONS, 2, longest - 1, longest),
        "coreg": (ITERATIONS, 2, longest),
    }
    for name, shape in counts.items():
        scratch[name + "_send"] = pltpu.SemaphoreType.DMA(shape)
        scratch[name + "_recv"] = pltpu.SemaphoreType.DMA(shape)
    operands = {
        "positions": positions.T,
        "field": object_field,
        "modes": probe.reshape(flat),
        "amplitude": amplitude,
        "tables": tables,
    }
    for name in STAGED:
        scratch["held_" + name] = pltpu.VMEM(operands[name].shape, operands[name].dtype)
    inputs = ["scan_list"] + list(STAGED)
    outputs = ["new_field", "new_modes"]
    names = inputs + outputs + list(scratch)
    in_vmem = pl.BlockSpec(memory_space=pltpu.VMEM)
    field, modes = pl.pallas_call(
        functools.partial(iterations_kernel, names, reach, chips_z, owners, PROBE_RATE / total),
        out_shape=(
            jax.ShapeDtypeStruct(object_field.shape, jnp.float32),
            jax.ShapeDtypeStruct(flat, jnp.float32),
        ),
        in_specs=[pl.BlockSpec(memory_space=pltpu.SMEM)]
        + [pl.BlockSpec(memory_space=pl.ANY)] * len(STAGED),
        out_specs=(in_vmem, in_vmem),
        scratch_shapes=list(scratch.values()),
        compiler_params=pltpu.CompilerParams(
            collective_id=1, has_side_effects=True, vmem_limit_bytes=VMEM_LIMIT
        ),
    )(scan_list, *[operands[name] for name in STAGED])
    field, modes = handed_over(field, modes)
    return field, modes.reshape(probe.shape)


def solution(mesh, chips_z=CHIPS_Z):
    in_specs = (
        P(None, "scan", "tile"),
        P(),
        P(("scan", "tile"), None, None),
        P(),
        P(("scan", "tile")),
    )
    out_specs = (P(None, "scan", "tile"), P())
    return jax.shard_map(
        functools.partial(on_device, chips_z),
        mesh=mesh,
        in_specs=in_specs,
        out_specs=out_specs,
        check_vma=False,
    )
```

```python
import functools
import math

import jax
import jax.numpy as jnp
import ml_dtypes
import numpy as np
from jax import lax
from jax.experimental import pallas as pl
from jax.experimental.pallas import tpu as pltpu
from jax.sharding import PartitionSpec as P

ITERATIONS = 2
INTENSITY_FLOOR = 0.1
OBJECT_RATE = 0.05
PROBE_RATE = 0.5

CORES = 2
CHIPS_Z = 8
LANES = 128
MESH = pl.DeviceIdType.MESH
STAGED = ("positions", "field", "modes", "amplitude", "tables")
VMEM_LIMIT = 56 * 1024 * 1024


def dft_tables(length):
    index = np.arange(length // 2)
    scale = 1.0 / math.sqrt(length)
    tables = []
    for parity in range(2):
        phase = np.outer(index, 2 * index + parity) % length
        angle = phase * (-2.0 * math.pi / length)
        cosine, sine = np.cos(angle) * scale, np.sin(angle) * scale
        forward = np.block([[cosine, sine], [-sine, cosine]])
        for table in (forward, forward.T):
            high = table.astype(ml_dtypes.bfloat16)
            low = (table - high.astype(np.float64)).astype(ml_dtypes.bfloat16)
            tables += [high, low]
    order = np.concatenate([np.arange(0, length, 2), np.arange(1, length, 2)])
    tables.append(np.eye(length)[:, order].astype(ml_dtypes.bfloat16))
    return np.stack(tables)


def halves(values):
    high = values.astype(jnp.bfloat16)
    low = (values - high.astype(jnp.float32)).astype(jnp.bfloat16)
    return high, low


def product(left, right):
    dot = functools.partial(jnp.dot, preferred_element_type=jnp.float32)
    return dot(left[0], right[0]) + (dot(left[0], right[1]) + dot(left[1], right[0]))


def permuted(values, order):
    total = None
    for _ in range(3):
        part = values.astype(jnp.bfloat16)
        values = values - part.astype(jnp.float32)
        moved = jnp.dot(part, order, preferred_element_type=jnp.float32)
        total = moved if total is None else total + moved
    return total


def beside(parts):
    return jnp.concatenate(parts, axis=1)


def stacked(parts):
    return jnp.concatenate(parts, axis=0)


class Place:
    def __init__(self, chips_z):
        self.scan = lax.axis_index("scan")
        self.tile = lax.axis_index("tile")
        self.scans = lax.axis_size("scan")
        self.tiles = lax.axis_size("tile")
        self.chips_z = chips_z
        self.chips_x = self.scans // (chips_z * CORES)
        self.core = lax.rem(self.scan, CORES)
        self.z = lax.rem(self.scan // CORES, chips_z)
        self.x = self.scan // (CORES * chips_z)

    def at_core(self):
        return (self.scan + 1 - 2 * self.core, self.tile)

    def ring_x(self, k):
        x = lax.rem(self.x + k, self.chips_x)
        return x, ((x * self.chips_z + self.z) * CORES + self.core, self.tile)

    def ring_z(self, k):
        z = lax.rem(self.z + k, self.chips_z)
        return z, ((self.x * self.chips_z + z) * CORES + self.core, self.tile)

    def ring(self, axis, k):
        return self.ring_x(k) if axis == "x" else self.ring_tile(k)

    def along(self, axis):
        return (self.x, self.chips_x) if axis == "x" else (self.tile, self.tiles)

    def ring_tile(self, k):
        tile = lax.rem(self.tile + k, self.tiles)
        return tile, (self.scan, tile)

    def near(self, d):
        other = self.scan + d
        return jnp.logical_and(other >= 0, other < self.scans), (other, self.tile)


def around(size):
    return sorted(range(1, size), key=lambda k: -min(k, size - k))


def distances(reach):
    far_first = sorted(range(1, reach + 1), reverse=True)
    return [sign * d for d in far_first for sign in (1, -1)]


def greet(partners):
    barrier = pltpu.get_barrier_semaphore()
    total = 0
    for condition, device in partners:
        if condition is None:
            pl.semaphore_signal(barrier, inc=1, device_id=device, device_id_type=MESH)
            total = total + 1
        else:

            @pl.when(condition)
            def _(device=device):
                pl.semaphore_signal(barrier, inc=1, device_id=device, device_id_type=MESH)

            total = total + condition.astype(jnp.int32)
    return lambda: pl.semaphore_wait(barrier, total)


def sublane(shape):
    return lax.broadcasted_iota(jnp.int32, shape, 1)


def read_patch(band, row, patch):
    groups, margin = patch // 8, (band.shape[0] - patch) // 8
    tiled = band.reshape(groups + margin, 8, band.shape[1])
    block, inside = row // 8, lax.rem(row, 8)
    values = tiled[: groups + 1]
    for q in range(1, margin):
        values = jnp.where(block == q, tiled[q : q + groups + 1], values)
    turned = pltpu.roll(values, lax.rem(8 - inside, 8), 1)
    values = jnp.where(sublane(turned[1:].shape) < 8 - inside, turned[:-1], turned[1:])
    return values.reshape(patch, band.shape[1])


def place_patch(values, row, margin):
    patch, width = values.shape
    groups, margin = patch // 8, margin // 8
    block, inside = row // 8, lax.rem(row, 8)
    turned = pltpu.roll(values.reshape(groups, 8, width), inside, 1)
    edge = jnp.zeros((1, 8, width), values.dtype)
    before = stacked([edge, turned])
    after = stacked([turned, edge])
    values = jnp.where(sublane(before.shape) < inside, before, after)
    pad = jnp.zeros((margin - 1, 8, width), values.dtype)
    padded = stacked([pad, values, pad])
    band = padded[margin - 1 :]
    for q in range(1, margin):
        start = margin - 1 - q
        band = jnp.where(block == q, padded[start : start + groups + margin], band)
    return band.reshape((groups + margin) * 8, width)


def slot_gradient(row, window, modes, patterns, tables, grad, grad_modes, patch_ref, slot):
    patch = patch_ref.shape[1]
    count = modes.shape[0] // (2 * patch)
    half = patch // 2
    straight = [(tables[4 * p], tables[4 * p + 1]) for p in range(2)]
    turned = [(tables[4 * p + 2], tables[4 * p + 3]) for p in range(2)]

    def rows_of(part, m):
        return slice((part * count + m) * patch, (part * count + m + 1) * patch)

    for part in range(2):
        patch_ref[part] = read_patch(window[part], row, patch)
    pieces = [[], []]
    for m in range(count):
        patch_real, patch_imag = patch_ref[0], patch_ref[1]
        mode_real, mode_imag = modes[rows_of(0, m), :], modes[rows_of(1, m), :]
        real = mode_real * patch_real - mode_imag * patch_imag
        imag = mode_real * patch_imag + mode_imag * patch_real
        pieces[0].append(beside([real[:, :half] + real[:, half:], imag[:, :half] + imag[:, half:]]))
        pieces[1].append(beside([real[:, :half] - real[:, half:], imag[:, :half] - imag[:, half:]]))
    columns = [product(halves(stacked(pieces[p])), straight[p]) for p in range(2)]
    far = [[], []]
    power = [None, None]
    for m in range(count):
        even, odd = (columns[p][m * patch : (m + 1) * patch] for p in range(2))
        real = beside([even[:, :half], odd[:, :half]])
        imag = beside([even[:, half:], odd[:, half:]])
        pieces = (
            stacked([real[:half] + real[half:], imag[:half] + imag[half:]]),
            stacked([real[:half] - real[half:], imag[:half] - imag[half:]]),
        )
        for p in range(2):
            value = product(turned[p], halves(pieces[p]))
            far[p].append(value)
            square = value[:half] * value[:half] + value[half:] * value[half:]
            power[p] = square if power[p] is None else power[p] + square
    factor = []
    for p in range(2):
        value = 1.0 - patterns[p] * lax.rsqrt(jnp.maximum(power[p], INTENSITY_FLOOR))
        factor.append(stacked([value, value]))
    pieces = [[], []]
    for m in range(count):
        even, odd = (product(straight[p], halves(far[p][m] * factor[p])) for p in range(2))
        upper, lower = even + odd, even - odd
        real = stacked([upper[:half], lower[:half]])
        imag = stacked([upper[half:], lower[half:]])
        pieces[0].append(beside([real[:, :half], imag[:, :half]]))
        pieces[1].append(beside([real[:, half:], imag[:, half:]]))
    columns = [product(halves(stacked(pieces[p])), turned[p]) for p in range(2)]
    term_real = term_imag = None
    for m in range(count):
        even, odd = (columns[p][m * patch : (m + 1) * patch] for p in range(2))
        upper, lower = even + odd, even - odd
        back_real = beside([upper[:, :half], lower[:, :half]])
        back_imag = beside([upper[:, half:], lower[:, half:]])
        patch_real, patch_imag = patch_ref[0], patch_ref[1]
        mode_real, mode_imag = modes[rows_of(0, m), :], modes[rows_of(1, m), :]
        real = mode_real * back_real + mode_imag * back_imag
        imag = mode_real * back_imag - mode_imag * back_real
        term_real = real if term_real is None else term_real + real
        term_imag = imag if term_imag is None else term_imag + imag
        probe_real = patch_real * back_real + patch_imag * back_imag
        probe_imag = patch_real * back_imag - patch_imag * back_real
        if slot == 0:
            grad_modes[rows_of(0, m), :] = probe_real
            grad_modes[rows_of(1, m), :] = probe_imag
        else:
            grad_modes[rows_of(0, m), :] += probe_real
            grad_modes[rows_of(1, m), :] += probe_imag
    margin = window.shape[1] - patch
    grad[0] = place_patch(term_real, row, margin)
    grad[1] = place_patch(term_imag, row, margin)


def rows_at(start, size):
    return pl.ds(pl.multiple_of(start, 8), size)


def iterations_kernel(names, reach, chips_z, owners, rate, *refs):
    at_name = dict(zip(names, refs))
    held = {name: at_name["held_" + name] for name in STAGED}
    first_field, first_modes = held["field"], held["modes"]
    amplitude, tables = held["amplitude"], held["tables"]
    notes_of, table = at_name["notes_of"], at_name["table"]
    place = Place(chips_z)
    _, rows, width = first_field.shape
    slots, patch = amplitude.shape[0], amplitude.shape[1]
    order = distances(reach)
    xs, ys, zs = place.chips_x, place.tiles, place.chips_z
    half = first_modes.shape[0] // CORES
    chains = (("x", "tile"), ("tile", "x"))
    chain = half // len(chains)
    part = chain // (xs * ys)
    piece = part // owners
    lane = lax.broadcasted_iota(jnp.int32, (rows, LANES), 1)
    blocks = width * ys // LANES
    wide = width // LANES
    finish = []

    def sems(name, *index):
        return at_name[name + "_send"].at[index], at_name[name + "_recv"].at[index]

    def copy_to(src, dst, device, name, *index):
        send, recv = sems(name, *index)
        return pltpu.make_async_remote_copy(
            src_ref=src, dst_ref=dst, send_sem=send, recv_sem=recv, device_id=device, device_id_type=MESH
        )

    def send(copy, condition=None):
        if condition is None:
            copy.start()
            finish.append(copy.wait_send)
        else:
            pl.when(condition)(copy.start)
            finish.append(lambda: pl.when(condition)(copy.wait_send))

    def owns(chain_at, z):
        return lax.rem(z + zs * len(chains) - chain_at * owners, zs)

    partners = [(None, place.at_core())]
    partners += [(None, place.ring_x(k)[1]) for k in range(1, xs)]
    partners += [(None, place.ring_tile(k)[1]) for k in range(1, ys)]
    for k in range(1, zs):
        z, device = place.ring_z(k)
        meets = functools.reduce(
            jnp.logical_or, [owns(c, at) < owners for c in range(len(chains)) for at in (z, place.z)]
        )
        partners.append((meets, device))
    partners += [place.near(d) for d in order]
    everyone_here = greet(partners)
    staged = {}
    for at, name in enumerate(STAGED):
        staged[name] = pltpu.make_async_copy(at_name[name], held[name], at_name["staged"].at[at])
        staged[name].start()

    def share_strip(it, field):
        strip = at_name["strip"].at[it]
        own = pl.ds(pl.multiple_of(place.tile * width, LANES), width)
        copies = []
        for k in around(ys):
            copy = copy_to(field, strip.at[:, :, own], place.ring_tile(k)[1], "strip", it, k - 1)
            send(copy)
            copies.append(copy)
        strip[:, :, own] = field[...]
        return copies

    def cut(it, source, slot, target):
        strip = at_name["strip"].at[it]
        column = notes_of[source, 1, slot]
        first = column // LANES
        inside = column - first * LANES
        for p in range(2):
            pieces = []
            for i in range(wide + 1):
                value = strip[p, :, LANES * i : LANES * (i + 1)]
                for block in range(1, blocks - wide + 1):
                    at = min(block + i, blocks - 1)
                    value = jnp.where(first == block, strip[p, :, LANES * at : LANES * (at + 1)], value)
                pieces.append(pltpu.roll(value, lax.rem(LANES - inside, LANES), 1))
            for i in range(wide):
                target[p, :, LANES * i : LANES * (i + 1)] = jnp.where(
                    lane < LANES - inside, pieces[i], pieces[i + 1]
                )

    def send_windows(it, slot):
        window = at_name["window"].at[it, slot]
        copies = []
        for at, d in enumerate(order):
            exists, device = place.near(d)
            outgoing = at_name["outgoing"].at[it, slot, at]
            copy = copy_to(
                outgoing, window.at[:, (reach - d) * rows : (reach - d + 1) * rows, :],
                device, "window", it, slot, at,
            )
            cut(it, reach + d, slot, outgoing)
            send(copy, exists)
            copies.append((place.near(-d)[0], copy))
        cut(it, reach, slot, window.at[:, reach * rows : (reach + 1) * rows, :])
        return copies

    def send_gradient(it, slot):
        grad = at_name["grad"].at[it, slot]
        arrived = at_name["arrived"].at[it, slot]
        copies = []
        for at, d in enumerate(order):
            exists, device = place.near(d)
            copy = copy_to(
                grad.at[:, (reach + d) * rows : (reach + d + 1) * rows, :], arrived.at[reach - d],
                device, "grad", it, slot, at,
            )
            send(copy, exists)
            copies.append((place.near(-d)[0], copy))
        arrived[reach] = grad[:, reach * rows : (reach + 1) * rows, :]
        return copies

    def place_windows(it, slot):
        strip = at_name["grad_strip"].at[it]
        arrived = at_name["arrived"].at[it, slot]

        def place_window(source, carry):
            column = notes_of[source, 1, slot]
            first = column // LANES
            inside = column - first * LANES
            for p in range(2):
                values = [
                    pltpu.roll(arrived[source, p, :, LANES * i : LANES * (i + 1)], inside, 1)
                    for i in range(wide)
                ]
                values = [jnp.zeros_like(values[0])] + values + [jnp.zeros_like(values[0])]
                shifted = [jnp.where(lane < inside, values[i], values[i + 1]) for i in range(wide + 1)]
                for block in range(blocks):
                    term = jnp.zeros_like(values[0])
                    for i, value in enumerate(shifted):
                        term = jnp.where(first + i == block, value, term)
                    strip[p, :, LANES * block : LANES * (block + 1)] += term
            return carry

        lax.fori_loop(0, 2 * reach + 1, place_window, 0)

    def wait_near(copies):
        for exists, copy in copies:
            pl.when(exists)(copy.wait_recv)

    for d in order:

        @pl.when(jnp.logical_not(place.near(-d)[0]))
        def _(d=d):
            table[reach - d] = jnp.zeros(table.shape[1:], jnp.int32)
            for it in range(ITERATIONS):
                for slot in range(slots):
                    at_name["window"][it, slot, :, (reach - d) * rows : (reach - d + 1) * rows, :] = (
                        jnp.zeros((2, rows, patch), jnp.float32)
                    )
                    at_name["arrived"][it, slot, reach - d] = jnp.zeros((2, rows, patch), jnp.float32)

    at_name["grad_strip"][...] = jnp.zeros(at_name["grad_strip"].shape, jnp.float32)
    staged["positions"].wait()
    position = held["positions"][...].astype(jnp.float32)
    index = lax.broadcasted_iota(jnp.int32, position.shape, 1)
    note_at = [lax.broadcasted_iota(jnp.int32, table.shape[1:], axis) for axis in range(2)]
    note = jnp.zeros(table.shape[1:], jnp.float32)
    for slot in range(slots):
        found = jnp.sum(jnp.where(index == at_name["scan_list"][slot], position, 0.0), axis=1, keepdims=True)
        for p in range(2):
            here = jnp.logical_and(note_at[0] == p, note_at[1] == slot)
            note = jnp.where(here, jnp.broadcast_to(found[p : p + 1], note.shape), note)
    table[reach] = note.astype(jnp.int32)
    staged["field"].wait()
    everyone_here()

    strip_copies = share_strip(0, first_field)
    notes = []
    for at, d in enumerate(order):
        exists, device = place.near(d)
        copy = copy_to(table.at[reach], table.at[reach - d], device, "note", at)
        send(copy, exists)
        notes.append((place.near(-d)[0], copy))
    wait_near(notes)
    local = pltpu.make_async_copy(table, notes_of, at_name["local"])
    local.start()
    local.wait()
    for copy in strip_copies:
        copy.wait_recv()
    window_copies = [send_windows(0, slot) for slot in range(slots)]
    for name in ("modes", "amplitude", "tables"):
        staged[name].wait()
    for slot in range(slots):
        pattern = permuted(amplitude[slot], tables[8])
        for q in range(2):
            at_name["pattern"][slot, q] = pattern[:, q * (patch // 2) : (q + 1) * (patch // 2)]
        for p in range(2):
            at_name["patterns"][slot, p] = beside(
                [at_name["pattern"][slot, q, pl.ds(p, patch // 2, stride=2), :] for q in range(2)]
            )

    for it in range(ITERATIONS):
        last = it == ITERATIONS - 1
        field = first_field if it == 0 else at_name["field_between"]
        modes = first_modes if it == 0 else at_name["modes_between"]
        new_field = at_name["new_field"] if last else at_name["field_between"]
        new_modes = at_name["new_modes"] if last else at_name["modes_between"]
        grad_modes = at_name["grad_modes"].at[it]

        grad_copies = []
        for slot in range(slots):
            wait_near(window_copies[slot])
            slot_gradient(
                notes_of[reach, 0, slot] - place.scan * rows + patch // 2, at_name["window"].at[it, slot], modes, at_name["patterns"].at[slot], tables,
                at_name["grad"].at[it, slot], grad_modes, at_name["patch"], slot,
            )
            if slot < slots - 1:
                grad_copies.append(send_gradient(it, slot))

        mine, other = place.core * half, (1 - place.core) * half
        core_part, core_sum = at_name["core_part"].at[it], at_name["core_sum"].at[it]
        core_copies = []
        for k in around(max(xs, ys)) + [max(xs, ys)]:
            for c, (axis, _) in enumerate(chains):
                here, size = place.along(axis)
                if k > size:
                    continue
                quarter = chain // size
                start = c * chain + lax.rem(here + k, size) * quarter
                copy = copy_to(
                    grad_modes.at[rows_at(other + start, quarter)], core_part.at[rows_at(start, quarter)],
                    place.at_core(), "core", it, c, k - 1,
                )
                send(copy)
                core_copies.append((c, axis, k, size, quarter, start, copy))
        grad_copies.append(send_gradient(it, slots - 1))
        one_copies = [[], []]
        for c, axis, k, size, quarter, start, copy in core_copies:
            copy.wait_recv()
            at = rows_at(start, quarter)
            core_sum[at, :] = core_part[at, :] + grad_modes[rows_at(mine + start, quarter), :]
            if k < size:
                here_two, size_two = place.along(chains[c][1])
                for which in around(size_two) + [0]:
                    offset = lax.rem(here_two + which, size_two) * part
                    copy = copy_to(
                        core_sum.at[rows_at(start + offset, part)],
                        at_name["one_parts"].at[it, c, k - 1, rows_at(offset, part)],
                        place.ring(axis, k)[1], "one", it, c, k - 1, which,
                    )
                    send(copy)
                    one_copies[c].append((which, copy))
        if not last:
            for slot in range(slots - 1):
                wait_near(grad_copies[slot])
                place_windows(it, slot)
        two_copies = [[], []]
        for c, (axis, axis_two) in enumerate(chains):
            here, size = place.along(axis)
            quarter = chain // size
            one_sum = at_name["one_sum"].at[it, c, pl.ds(0, quarter)]
            for k in around(place.along(axis_two)[1]) + [0]:
                for which, copy in one_copies[c]:
                    if which == k:
                        copy.wait_recv()
                to, device = place.ring(axis_two, k)
                at = rows_at(to * part, part)
                total = core_sum[rows_at(c * chain + here * quarter + to * part, part), :]
                for i in range(size - 1):
                    total = total + at_name["one_parts"][it, c, i, at, :]
                one_sum[at, :] = total
                if k == 0:
                    continue
                copy = copy_to(
                    one_sum.at[rows_at(to * part, part)], at_name["two_parts"].at[it, c, k - 1],
                    device, "two", it, c, k - 1,
                )
                send(copy)
                two_copies[c].append(copy)

        grad_strip = at_name["grad_strip"].at[it]
        tile_copies = []

        def sum_windows(slot_range):
            for slot in slot_range:
                wait_near(grad_copies[slot])
                place_windows(it, slot)
            for k in around(ys):
                y, device = place.ring_tile(k)
                copy = copy_to(
                    grad_strip.at[:, :, pl.ds(pl.multiple_of(y * width, LANES), width)],
                    at_name["tile_parts"].at[it, k - 1], device, "tile", it, k - 1,
                )
                send(copy)
                tile_copies.append(copy)

        def update_field():
            for copy in tile_copies:
                copy.wait_recv()
            total = grad_strip[:, :, pl.ds(pl.multiple_of(place.tile * width, LANES), width)]
            for k in range(ys - 1):
                total = total + at_name["tile_parts"][it, k]
            new_field[...] = field[...] - OBJECT_RATE * total

        if not last:
            sum_windows(range(slots - 1, slots))
        z_copies = [[], []]
        for c, (_, axis_two) in enumerate(chains):
            here, size = place.along(axis_two)
            for copy in two_copies[c]:
                copy.wait_recv()
            total = at_name["one_sum"][it, c, rows_at(here * part, part), :]
            for k in range(size - 1):
                total = total + at_name["two_parts"][it, c, k]
            two_sum = at_name["two_sum"].at[it, c]
            two_sum[...] = total
            for k in around(zs):
                z, device = place.ring_z(k)
                owned = owns(c, z)
                copy = copy_to(
                    two_sum.at[rows_at(jnp.minimum(owned, owners - 1) * piece, piece)],
                    at_name["z_parts"].at[it, c, k - 1], device, "z", it, c, k - 1,
                )
                send(copy, owned < owners)
                z_copies[c].append(copy)

        if last:
            sum_windows(range(slots))
        else:
            update_field()
            strip_copies = share_strip(it + 1, new_field)

        my_quarters, my_parts, zg_copies = [], [], [[], []]
        for c, (axis, axis_two) in enumerate(chains):
            here, size = place.along(axis)
            my_quarter = mine + c * chain + here * (chain // size)
            my_part = my_quarter + place.along(axis_two)[0] * part
            my_quarters.append(my_quarter)
            my_parts.append(my_part)
            owned = owns(c, place.z)
            owner = owned < owners
            my_piece = jnp.minimum(owned, owners - 1) * piece

            @pl.when(owner)
            def _(c=c, my_part=my_part, my_piece=my_piece):
                for copy in z_copies[c]:
                    copy.wait_recv()
                total = at_name["two_sum"][it, c, rows_at(my_piece, piece), :]
                for k in range(zs - 1):
                    total = total + at_name["z_parts"][it, c, k]
                at = rows_at(my_part + my_piece, piece)
                new_modes[at, :] = modes[at, :] - rate * total

            for k in around(zs):
                ref = new_modes.at[rows_at(my_part + my_piece, piece)]
                copy = copy_to(ref, ref, place.ring_z(k)[1], "zg", it, c, k - 1)
                send(copy, owner)
                zg_copies[c].append((owns(c, lax.rem(place.z + zs - k, zs)) < owners, copy))
        two_copies = [[], []]
        one_copies, core_copies = [{}, {}], []

        def pass_on(c, which, start):
            axis = chains[c][0]
            ref = new_modes.at[rows_at(start, part)]
            for k in around(place.along(axis)[1]):
                copy = copy_to(ref, ref, place.ring(axis, k)[1], "oneg", it, c, k - 1, which)
                send(copy)
                one_copies[c][k, which] = copy

        for c, (_, axis_two) in enumerate(chains):
            wait_near(zg_copies[c])
            for k in around(place.along(axis_two)[1]):
                ref = new_modes.at[rows_at(my_parts[c], part)]
                copy = copy_to(ref, ref, place.ring(axis_two, k)[1], "twog", it, c, k - 1)
                send(copy)
                two_copies[c].append((k, copy))
            pass_on(c, 0, my_parts[c])
        if last:
            update_field()
        else:
            for copy in strip_copies:
                copy.wait_recv()
            window_copies = [send_windows(it + 1, 0)]
        for c, (axis, axis_two) in enumerate(chains):
            here_two, size_two = place.along(axis_two)
            for k, copy in reversed(two_copies[c]):
                copy.wait_recv()
                pass_on(c, k, my_quarters[c] + lax.rem(here_two + size_two - k, size_two) * part)
            here, size = place.along(axis)
            quarter = chain // size
            ref = new_modes.at[rows_at(my_quarters[c], quarter)]
            copy = copy_to(ref, ref, place.at_core(), "coreg", it, c, 0)
            send(copy)
            core_copies.append(copy)
        if not last:
            window_copies += [send_windows(it + 1, slot) for slot in range(1, slots)]
        for k in around(max(xs, ys))[::-1]:
            for c, (axis, _) in enumerate(chains):
                here, size = place.along(axis)
                if k >= size:
                    continue
                for which in range(place.along(chains[c][1])[1]):
                    one_copies[c][k, which].wait_recv()
                quarter = chain // size
                start = mine + c * chain + lax.rem(here + size - k, size) * quarter
                ref = new_modes.at[rows_at(start, quarter)]
                copy = copy_to(ref, ref, place.at_core(), "coreg", it, c, k)
                send(copy)
                core_copies.append(copy)
        for copy in core_copies:
            copy.wait_recv()
    for wait in finish:
        wait()


def hand_over_kernel(field_ref, modes_ref, field_out, modes_out, sems):
    copies = [
        pltpu.make_async_copy(field_ref, field_out, sems.at[0]),
        pltpu.make_async_copy(modes_ref, modes_out, sems.at[1]),
    ]
    for copy in copies:
        copy.start()
    for copy in copies:
        copy.wait()


def handed_over(field, modes):
    vmem, anywhere = pl.BlockSpec(memory_space=pltpu.VMEM), pl.BlockSpec(memory_space=pl.ANY)
    return pl.pallas_call(
        hand_over_kernel,
        out_shape=(
            jax.ShapeDtypeStruct(field.shape, jnp.float32),
            jax.ShapeDtypeStruct(modes.shape, jnp.float32),
        ),
        in_specs=[vmem, vmem],
        out_specs=(anywhere, anywhere),
        scratch_shapes=[pltpu.SemaphoreType.DMA((2,))],
    )(field, modes)


def on_device(chips_z, object_field, probe, amplitude, positions, scan_list):
    _, rows, width = object_field.shape
    patch = probe.shape[2]
    reach = patch // (2 * rows)
    near = 2 * reach
    total = positions.shape[0]
    slots = scan_list.shape[0]
    tiles, scans = lax.axis_size("tile"), lax.axis_size("scan")
    chips_x = scans // (CORES * chips_z)
    flat = (probe.size // patch, patch)
    half = flat[0] // CORES
    chain = half // 2
    part = chain // (chips_x * tiles)
    owners = max(n for n in range(1, chips_z + 1) if part % (8 * n) == 0)
    piece = part // owners
    longest = max(chips_x, tiles)
    quarter = chain // min(chips_x, tiles)

    tables = jnp.asarray(dft_tables(patch))

    def vmem(*shape):
        return pltpu.VMEM((ITERATIONS,) + shape, jnp.float32)

    band = (2, (near + 1) * rows, patch)
    block = (2, rows, patch)
    scratch = {
        "notes_of": pltpu.SMEM((near + 1, 8, LANES), jnp.int32),
        "table": pltpu.VMEM((near + 1, 8, LANES), jnp.int32),
        "strip": vmem(2, rows, width * tiles),
        "outgoing": vmem(slots, near, *block),
        "window": vmem(slots, *band),
        "grad": vmem(slots, *band),
        "arrived": vmem(slots, near + 1, *block),
        "grad_strip": vmem(2, rows, width * tiles),
        "tile_parts": vmem(tiles - 1, 2, rows, width),
        "field_between": pltpu.VMEM(object_field.shape, jnp.float32),
        "modes_between": pltpu.VMEM(flat, jnp.float32),
        "patch": pltpu.VMEM((2, patch, patch), jnp.float32),
        "pattern": pltpu.VMEM((slots, 2, patch, patch // 2), jnp.float32),
        "patterns": pltpu.VMEM((slots, 2, patch // 2, patch), jnp.float32),
        "grad_modes": vmem(*flat),
        "core_part": vmem(half, patch),
        "core_sum": vmem(half, patch),
        "one_parts": vmem(2, longest - 1, quarter, patch),
        "one_sum": vmem(2, quarter, patch),
        "two_parts": vmem(2, longest - 1, part, patch),
        "two_sum": vmem(2, part, patch),
        "z_parts": vmem(2, chips_z - 1, piece, patch),
        "local": pltpu.SemaphoreType.DMA(()),
        "staged": pltpu.SemaphoreType.DMA((len(STAGED),)),
    }
    counts = {
        "note": (near,),
        "strip": (ITERATIONS, tiles - 1),
        "window": (ITERATIONS, slots, near),
        "grad": (ITERATIONS, slots, near),
        "tile": (ITERATIONS, tiles - 1),
        "core": (ITERATIONS, 2, longest),
        "one": (ITERATIONS, 2, longest - 1, longest),
        "two": (ITERATIONS, 2, longest - 1),
        "z": (ITERATIONS, 2, chips_z - 1),
        "zg": (ITERATIONS, 2, chips_z - 1),
        "twog": (ITERATIONS, 2, longest - 1),
        "oneg": (ITERATIONS, 2, longest - 1, longest),
        "coreg": (ITERATIONS, 2, longest),
    }
    for name, shape in counts.items():
        scratch[name + "_send"] = pltpu.SemaphoreType.DMA(shape)
        scratch[name + "_recv"] = pltpu.SemaphoreType.DMA(shape)
    operands = {
        "positions": positions.T,
        "field": object_field,
        "modes": probe.reshape(flat),
        "amplitude": amplitude,
        "tables": tables,
    }
    for name in STAGED:
        scratch["held_" + name] = pltpu.VMEM(operands[name].shape, operands[name].dtype)
    inputs = ["scan_list"] + list(STAGED)
    outputs = ["new_field", "new_modes"]
    names = inputs + outputs + list(scratch)
    in_vmem = pl.BlockSpec(memory_space=pltpu.VMEM)
    field, modes = pl.pallas_call(
        functools.partial(iterations_kernel, names, reach, chips_z, owners, PROBE_RATE / total),
        out_shape=(
            jax.ShapeDtypeStruct(object_field.shape, jnp.float32),
            jax.ShapeDtypeStruct(flat, jnp.float32),
        ),
        in_specs=[pl.BlockSpec(memory_space=pltpu.SMEM)]
        + [pl.BlockSpec(memory_space=pl.ANY)] * len(STAGED),
        out_specs=(in_vmem, in_vmem),
        scratch_shapes=list(scratch.values()),
        compiler_params=pltpu.CompilerParams(
            collective_id=1, has_side_effects=True, vmem_limit_bytes=VMEM_LIMIT
        ),
    )(scan_list, *[operands[name] for name in STAGED])
    field, modes = handed_over(field, modes)
    return field, modes.reshape(probe.shape)


def solution(mesh, chips_z=CHIPS_Z):
    in_specs = (
        P(None, "scan", "tile"),
        P(),
        P(("scan", "tile"), None, None),
        P(),
        P(("scan", "tile")),
    )
    out_specs = (P(None, "scan", "tile"), P())
    return jax.shard_map(
        functools.partial(on_device, chips_z),
        mesh=mesh,
        in_specs=in_specs,
        out_specs=out_specs,
        check_vma=False,
    )
```
